512 devices in a mesh: ctx: 32 (over x, z), hg: 16 (over y, core).
Axes of the slice: x: 4, y: 8, z: 8, core: 2. Of those that a mesh axis runs over, the one named last changes fastest.
Arguments:
- query_nope: bfloat16 [128, 128, 128], P('ctx', 'hg'), may hold values from -6 to 6
- query_rope: bfloat16 [128, 128, 64], P('ctx', 'hg'), may hold values from -160 to 160
- latent: bfloat16 [24576, 512], P('ctx'), may hold values from -6 to 6
- key_rope: bfloat16 [24576, 64], P('ctx'), may hold values from -160 to 160
- up_keys: bfloat16 [512, 128, 128], P(None, 'hg'), may hold values from -0.25 to 0.25
- up_values: bfloat16 [512, 128, 128], P(None, 'hg'), may hold values from -0.25 to 0.25
- out_weight: bfloat16 [128, 128, 7168], P('hg', None, 'ctx'), may hold values from -0.046875 to 0.046875
- live_rows: int32 [32], P('ctx'), may hold values from 1 to 768, 18432 in all
- span_start: int32 [1], replicated, may hold values from 9216 to 18304
Outputs:
- mixed: bfloat16 [128, 7168], P('hg', 'ctx')
The draws below stay inside these ranges and needn't reach their ends.
Inputs may be any that keep to these rules, and one draw needn't show every extreme that they name: `live_rows`: the values sum to 18432.
All inputs are finite; a program needn't handle non-finite values. No bound on the sum of `live_rows` on one device may be relied on, other than what follows from the above.
Results may differ from the reference program's by a relative error of at most 0.0082.
Values may be sent and summed in bfloat16 or wider, within the bound.
A program may use at most 64 MiB of HBM per device.

```python
import math
import jax
import jax.numpy as jnp
import numpy as np
from jax import lax

D = 7168
HEADS = 128
NOPE = 128
ROPE = 64
VDIM = 128
LAT = 512
QT = 128
KEY_DEV = 768
CTX = 24576
VTOTAL = 18432
N_CTX = 32


def draw_query_rope(key, part):
    key = jax.random.fold_in(key, 11)
    drawn = jax.random.normal(key, (QT, HEADS, ROPE), jnp.float32)
    return jnp.clip(drawn, -160.0, 160.0).astype(jnp.bfloat16)


def draw_key_rope(key, part):
    key = jax.random.fold_in(key, 23)
    drawn = jax.random.normal(key, (CTX, ROPE), jnp.float32)
    return jnp.clip(drawn, -160.0, 160.0).astype(jnp.bfloat16)


def level_of(own_key, shape, shards, smallest, largest):
    level = 1.0
    for position, blocks in shards:
        heights = jax.random.uniform(jax.random.fold_in(jax.random.fold_in(own_key, 6), position), (blocks,), jnp.float32, smallest / len(shards), largest / len(shards))
        level = level * jnp.repeat(jnp.exp(heights), shape[position] // blocks).reshape((-1,) + (1,) * (len(shape) - 1 - position))
    return level


def profile(count, total, reach, skew):
    weights = [(1 << 20) // math.isqrt(rank ** skew) + 1 for rank in range(2, count + 1)]
    rest, counts = total - reach - (count - 1), [1] * (count - 1)
    while rest > 0:
        candidates = [i for i in range(count - 1) if counts[i] < reach]
        whole, budget = sum([weights[i] for i in candidates]), rest
        for i in candidates:
            more = min(reach - counts[i], max(1, budget * weights[i] // whole), rest)
            counts[i] = counts[i] + more
            rest = rest - more
    return np.array([reach] + counts)


def ragged(key, count, total, limit, slope):
    if count == 2:
        one = jax.random.randint(key, (), max(1, total - limit), min(limit, total - 1) + 1)
        return jnp.stack([one, total - one])
    sizes = jnp.asarray(profile(count, total, limit, slope), jnp.int32)
    couples = (count - 1) // 2
    source_of, taker = sizes[1:1 + 2 * couples:2], sizes[2:2 + 2 * couples:2]
    margin = jnp.minimum(source_of - 1, limit - taker)
    moved = jax.random.randint(jax.random.fold_in(key, 1), (couples,), 0, 1 << 20) % (margin + 1)
    sizes = sizes.at[1:1 + 2 * couples:2].set(source_of - moved).at[2:2 + 2 * couples:2].set(taker + moved)
    return sizes[jax.random.permutation(jax.random.fold_in(key, 2), count)]


def gaussian(rng, dims, scale, reach, split=(), held_as=jnp.bfloat16):
    result = jax.random.normal(rng, dims, jnp.float32) * scale
    if len(split) > 0:
        result = level_of(rng, dims, split, -0.22, 0.18) * result
    return jnp.clip(result, min=-reach, max=reach).astype(held_as)


def setup_inputs(seed: int = 0) -> dict:
    keys = jax.random.split(jax.random.key(seed), 10)
    return {
        "query_nope": gaussian(keys[0], (QT, HEADS, NOPE), 1.0, 6.0, ((0, 32), (1, 16))),
        "query_rope": draw_query_rope(jax.random.fold_in(keys[9], 71), 0),
        "latent": gaussian(keys[2], (CTX, LAT), 1.0, 6.0, ((0, 32),)),
        "key_rope": draw_key_rope(jax.random.fold_in(keys[9], 71), 0),
        "up_keys": gaussian(keys[4], (LAT, HEADS, NOPE), LAT ** -0.5, 0.25, ((1, 16),)),
        "up_values": gaussian(keys[5], (LAT, HEADS, VDIM), LAT ** -0.5, 0.25, ((1, 16),)),
        "out_weight": gaussian(keys[6], (HEADS, VDIM, D), (HEADS * VDIM) ** -0.5, 0.046875, ((0, 16), (2, 32))),
        "live_rows": ragged(keys[7], N_CTX, VTOTAL, KEY_DEV, 2).astype(jnp.int32),
        "span_start": jax.random.randint(keys[8], (1,), VTOTAL // 2, VTOTAL - QT + 1).astype(jnp.int32),
    }


NEG = -1e+30

def attend_shard(query_nope, query_rope, latent, key_rope, up_keys, up_values, positions, offset, count):
    key_block = jnp.einsum('jl,lhd->jhd', latent.astype(jnp.float32), up_keys.astype(jnp.float32)).astype(jnp.bfloat16)
    value_block = jnp.einsum('jl,lhd->jhd', latent.astype(jnp.float32), up_values.astype(jnp.float32)).astype(jnp.bfloat16)
    factor = 1.0 / math.sqrt(query_nope.shape[-1] + query_rope.shape[-1])
    scores = jnp.einsum('ihd,jhd->hij', query_nope.astype(jnp.float32), key_block.astype(jnp.float32))
    scores = (scores + jnp.einsum('ihd,jd->hij', query_rope.astype(jnp.float32), key_rope.astype(jnp.float32))) * factor
    index = jnp.arange(latent.shape[0], dtype=jnp.int32)
    visible = (index < count)[None, :] & ((offset + index)[None, :] <= positions[:, None])
    scores = jnp.where(visible[None], scores, NEG)
    maxima = lax.optimization_barrier(jnp.max(scores, axis=2))
    weights = jnp.where(visible[None], jnp.exp(scores - maxima[:, :, None]), 0.0)
    totals = lax.optimization_barrier(jnp.sum(weights, axis=2))
    rounded = lax.optimization_barrier(weights.astype(jnp.bfloat16)).astype(jnp.float32)
    output = jnp.einsum('hij,jhd->ihd', rounded, value_block.astype(jnp.float32))
    return (maxima.T, totals.T, output)

def reference(query_nope, query_rope, latent, key_rope, up_keys, up_values, out_weight, live_rows, span_start):
    offsets = (jnp.cumsum(live_rows) - live_rows).astype(jnp.int32)
    positions = (span_start[0] + jnp.arange(QT, dtype=jnp.int32)).astype(jnp.int32)

    def visit(carry, shard):
        maxima, totals, output = carry
        first = (shard * KEY_DEV).astype(jnp.int32)
        lat_block = lax.dynamic_slice_in_dim(latent, first, KEY_DEV, 0)
        rope_block = lax.dynamic_slice_in_dim(key_rope, first, KEY_DEV, 0)
        part_max, part_tot, part_out = attend_shard(query_nope, query_rope, lat_block, rope_block, up_keys, up_values, positions, offsets[shard], live_rows[shard])
        joined = jnp.maximum(maxima, part_max)
        before = jnp.exp(maxima - joined)
        after = jnp.exp(part_max - joined)
        return ((joined, totals * before + part_tot * after, output * before[:, :, None] + part_out * after[:, :, None]), None)
    start_state = (jnp.full((QT, HEADS), NEG, jnp.float32), jnp.zeros((QT, HEADS), jnp.float32), jnp.zeros((QT, HEADS, VDIM), jnp.float32))
    final, unused = lax.scan(visit, start_state, jnp.arange(N_CTX, dtype=jnp.int32))
    maxima, totals, output = final
    attn = (output / totals[:, :, None]).astype(jnp.bfloat16).reshape(QT, HEADS * VDIM)
    return jnp.dot(attn, out_weight.reshape(HEADS * VDIM, D), preferred_element_type=jnp.float32).astype(jnp.bfloat16)
```

```python
import functools
import math

import jax
import jax.numpy as jnp
from jax import lax
from jax.experimental import pallas as pl
from jax.experimental.pallas import tpu as pltpu
from jax.sharding import PartitionSpec as P

NEG = -1e30
NCTX, NX, NZ, NHG = 32, 4, 8, 16
TOK, HD, DIM, ROPE, LAT, SLOTS, COLS = 128, 8, 128, 64, 512, 768, 224
FACTOR = 1.0 / math.sqrt(DIM + ROPE)
MESH = pl.DeviceIdType.MESH
F32, BF16 = jnp.float32, jnp.bfloat16


def rows(start, size, step=16):
    return pl.ds(pl.multiple_of(start, step), size)


def kernel(
    live, span, qn, qr, latent, rope_t, up_k, up_v, weight_t, out,
    lat_v, rope_v, upk_v, upv_v, wt_v, wide, wk, wvt, keys, values_t, kr,
    q_all, q_wide, o_mine, st_mine, o_all, st_all, a_all, part, part_all,
    load_sem, q_send, q_recv_z, q_recv_x, o_send, o_recv, st_send, st_recv,
    a_send, a_recv, p_send, p_recv,
):
    c, g = lax.axis_index("ctx"), lax.axis_index("hg")
    z = lax.rem(c, NZ)
    column = c - z

    def z_peer(k):
        return column + lax.rem(z + k, NZ)

    def x_peer(k):
        return lax.rem(c + NZ * k, NCTX)

    def h_peer(k):
        return lax.rem(g + k, NHG)

    def send(src, dst, send_sem, recv_sem, ctx, hg):
        pltpu.make_async_remote_copy(
            src_ref=src, dst_ref=dst, send_sem=send_sem, recv_sem=recv_sem,
            device_id=(ctx, hg), device_id_type=MESH,
        ).start()

    def drain(ref, sem):
        pltpu.make_async_copy(ref, ref, sem).wait()

    barrier = pltpu.get_barrier_semaphore()
    for k in range(1, NZ):
        pl.semaphore_signal(barrier, inc=1, device_id=(z_peer(k), g), device_id_type=MESH)
    for k in range(1, NX):
        pl.semaphore_signal(barrier, inc=1, device_id=(x_peer(k), g), device_id_type=MESH)
    for k in range(1, NHG):
        pl.semaphore_signal(barrier, inc=1, device_id=(c, h_peer(k)), device_id_type=MESH)

    loads = [
        pltpu.make_async_copy(src, dst, load_sem.at[i])
        for i, (src, dst) in enumerate(
            ((up_k, upk_v), (latent, lat_v), (up_v, upv_v), (rope_t, rope_v), (weight_t, wt_v))
        )
    ]
    for load in loads:
        load.start()

    count = live[0]
    nope = qn[...].astype(F32).reshape(4 * HD, DIM)
    rope = qr[...].astype(F32).reshape(4 * HD, ROPE)
    rope = jnp.concatenate([rope, jnp.zeros((4 * HD, DIM - ROPE), F32)], axis=1)
    lane = lax.broadcasted_iota(jnp.int32, (4 * HD, DIM), 1)
    high = lax.shift_right_logical(count, 3)
    low = count - high * 8
    rope = jnp.where(lane == ROPE, high.astype(F32), rope)
    rope = jnp.where(lane == ROPE + 1, low.astype(F32), rope)
    mine = rows(c * 32, 32)
    q_all[mine, 0:DIM] = nope.astype(BF16)
    q_all[mine, DIM:] = rope.astype(BF16)

    pl.semaphore_wait(barrier, (NZ - 1) + (NX - 1) + (NHG - 1))

    for k in (4, 3, 5, 2, 6, 1, 7):
        send(q_all.at[mine], q_all.at[mine], q_send, q_recv_z.at[k], z_peer(k), g)
    for j in (2, 1, 3):
        send(q_all.at[mine], q_all.at[mine], q_send, q_recv_x, x_peer(j), g)

    loads[0].wait()
    wide[...] = upk_v[...].astype(F32).reshape(LAT * HD, DIM)
    for h in range(HD):
        wk[:, h * DIM : (h + 1) * DIM] = wide[pl.ds(h, LAT, stride=HD), :].astype(BF16)
    loads[1].wait()
    for h in range(0, HD, 2):
        both = jnp.dot(
            lat_v[...], wk[:, h * DIM : (h + 2) * DIM], preferred_element_type=F32
        ).astype(BF16)
        keys[h] = both[:, 0:DIM]
        keys[h + 1] = both[:, DIM:]

    for k in (1, 7, 2, 6, 3, 5, 4):
        block = rows(z_peer(k) * 32, 32)
        drain(q_all.at[block], q_recv_z.at[NZ - k])
        for j in (2, 1, 3):
            send(q_all.at[block], q_all.at[block], q_send, q_recv_x, x_peer(j), g)

    loads[2].wait()
    wide[...] = upv_v[...].astype(F32).reshape(LAT * HD, DIM)
    for h in range(HD):
        wvt[h * DIM : (h + 1) * DIM, :] = wide[pl.ds(h, LAT, stride=HD), :].T.astype(BF16)
    for n in range(0, SLOTS, 256):
        values_t[:, n : n + 256] = lax.dot_general(
            wvt[...], lat_v[n : n + 256, :], (((1,), (1,)), ((), ())),
            preferred_element_type=F32,
        ).astype(BF16)
    loads[3].wait()
    kr[...] = jnp.concatenate(
        [rope_v[...].astype(F32), jnp.zeros((DIM - ROPE, SLOTS), F32)], axis=0
    ).T.astype(BF16)

    drain(q_all.at[pl.ds(0, 24 * 32)], q_recv_x)
    q_wide[0] = q_all[:, 0:DIM].astype(F32)
    q_wide[1] = q_all[:, DIM:].astype(F32)
    counts = q_wide[1, pl.ds(0, NCTX, stride=32), :]
    lane = lax.broadcasted_iota(jnp.int32, (NCTX, DIM), 1)
    shard = lax.broadcasted_iota(jnp.int32, (NCTX, DIM), 0)
    scale = jnp.where(lane == ROPE, 8.0, jnp.where(lane == ROPE + 1, 1.0, 0.0))
    before = jnp.where(shard < c, counts * scale, 0.0)
    offset = jnp.sum(jnp.sum(before, axis=0, keepdims=True), axis=1, keepdims=True)
    offset = offset.astype(jnp.int32)
    token = lax.broadcasted_iota(jnp.int32, (1, TOK), 1)
    limit = jnp.minimum(token + (span[0] + 1) - offset, count)
    slot = lax.broadcasted_iota(jnp.int32, (SLOTS, TOK), 0)
    visible = slot < limit

    own = lax.div(c, 4)
    for t in range(HD):
        h = lax.rem(own + 1 + t, HD)
        q = jnp.concatenate(
            [q_wide[i, pl.ds(h, TOK, stride=HD), :].astype(BF16) for i in range(2)], axis=1
        )
        k_cat = jnp.concatenate([keys[h], kr[...]], axis=1)
        scores = lax.dot_general(
            k_cat, q, (((1,), (1,)), ((), ())), preferred_element_type=F32
        )
        scores = jnp.where(visible, scores, NEG)
        top = jnp.max(scores, axis=0, keepdims=True)
        p = jnp.exp((scores - top) * FACTOR)
        st_mine[h, 0:1, :] = top
        st_mine[h, 1:2, :] = jnp.sum(p, axis=0, keepdims=True)
        feats = rows(h * DIM, DIM, DIM)
        o_mine[feats, :] = jnp.dot(
            values_t[feats, :], p.astype(BF16), preferred_element_type=F32
        ).astype(BF16)
        for j in range(4) if t < HD - 1 else range(1, 4):
            dst = 4 * h + (j if t < HD - 1 else lax.rem(c + j, 4))
            place = lax.rem(c - dst + NCTX, NCTX)
            send(
                o_mine.at[rows(dst * 32, 32)], o_all.at[rows(place * 32, 32)],
                o_send, o_recv, dst, g,
            )
            send(st_mine.at[h], st_all.at[place], st_send, st_recv, dst, g)

    o_all[0:32, :] = o_mine[mine, :]
    st_all[0] = st_mine[own]
    drain(st_all.at[pl.ds(1, NCTX - 1)], st_recv)
    drain(o_all.at[pl.ds(32, (NCTX - 1) * 32)], o_recv)
    tops = st_all[:, 0, :]
    weights = jnp.exp((tops - jnp.max(tops, axis=0, keepdims=True)) * FACTOR)
    total = jnp.sum(weights * st_all[:, 1, :], axis=0, keepdims=True)
    joined = jnp.zeros((32, TOK), F32)
    for s in range(NCTX):
        joined = joined + o_all[s * 32 : (s + 1) * 32, :].astype(F32) * weights[s : s + 1, :]
    a_all[mine, :] = (joined / total).astype(BF16)
    for k in range(1, NCTX):
        send(a_all.at[mine], a_all.at[mine], a_send, a_recv, lax.rem(c + k, NCTX), g)

    loads[4].wait()
    w = jnp.concatenate([wt_v[h] for h in range(HD)], axis=1)
    drain(a_all.at[pl.ds(0, (NCTX - 1) * 32)], a_recv)
    mixed_t = jnp.dot(w, a_all[...], preferred_element_type=F32)
    mixed_t = jnp.concatenate([mixed_t, jnp.zeros((256 - COLS, TOK), F32)], axis=0)
    left = mixed_t[0:128].T.reshape(NHG, 8, 128)
    right = mixed_t[128:].T.reshape(NHG, 8, 128)
    part[...] = jnp.concatenate([left, right], axis=1).astype(BF16).reshape(NHG * 16, 128)
    for k in range(1, NHG):
        send(
            part.at[rows(h_peer(k) * 16, 16)], part_all.at[pl.ds((NHG - k) * 16, 16)],
            p_send, p_recv, c, h_peer(k),
        )
    acc = part[rows(g * 16, 16), :].astype(F32)
    drain(part_all.at[pl.ds(16, (NHG - 1) * 16)], p_recv)
    for k in range(1, NHG):
        acc = acc + part_all[k * 16 : (k + 1) * 16, :].astype(F32)
    out[...] = jnp.concatenate([acc[0:8], acc[8:16, 0 : COLS - 128]], axis=1).astype(BF16)

    drain(q_all.at[pl.ds(0, 31 * 32)], q_send)
    drain(o_all.at[pl.ds(32, (NCTX - 1) * 32)], o_send)
    drain(st_all.at[pl.ds(1, NCTX - 1)], st_send)
    drain(a_all.at[pl.ds(0, (NCTX - 1) * 32)], a_send)
    drain(part_all.at[pl.ds(16, (NHG - 1) * 16)], p_send)


def per_device(
    query_nope, query_rope, latent, key_rope, up_keys, up_values, out_weight, live_rows, span_start
):
    anywhere = pl.BlockSpec(memory_space=pl.ANY)
    vmem = pl.BlockSpec(memory_space=pltpu.VMEM)
    smem = pl.BlockSpec(memory_space=pltpu.SMEM)
    dma = pltpu.SemaphoreType.DMA
    return pl.pallas_call(
        kernel,
        out_shape=jax.ShapeDtypeStruct((TOK // NHG, COLS), BF16),
        in_specs=[smem, smem, vmem, vmem] + [anywhere] * 5,
        out_specs=vmem,
        scratch_shapes=[
            pltpu.VMEM((SLOTS, LAT), BF16),
            pltpu.VMEM((ROPE, SLOTS), BF16),
            pltpu.VMEM((LAT, HD, DIM), BF16),
            pltpu.VMEM((LAT, HD, DIM), BF16),
            pltpu.VMEM((HD, COLS, DIM), BF16),
            pltpu.VMEM((LAT * HD, DIM), F32),
            pltpu.VMEM((LAT, HD * DIM), BF16),
            pltpu.VMEM((HD * DIM, LAT), BF16),
            pltpu.VMEM((HD, SLOTS, DIM), BF16),
            pltpu.VMEM((HD * DIM, SLOTS), BF16),
            pltpu.VMEM((SLOTS, DIM), BF16),
            pltpu.VMEM((TOK * HD, 2 * DIM), BF16),
            pltpu.VMEM((2, TOK * HD, DIM), F32),
            pltpu.VMEM((HD * DIM, TOK), BF16),
            pltpu.VMEM((HD, 2, TOK), F32),
            pltpu.VMEM((NCTX * 32, TOK), BF16),
            pltpu.VMEM((NCTX, 2, TOK), F32),
            pltpu.VMEM((HD * DIM, TOK), BF16),
            pltpu.VMEM((NHG * 16, 128), BF16),
            pltpu.VMEM((NHG * 16, 128), BF16),
            dma((5,)), dma, dma((NZ,)), dma, dma, dma, dma, dma, dma, dma, dma, dma,
        ],
        compiler_params=pltpu.CompilerParams(
            collective_id=0, has_side_effects=True, vmem_limit_bytes=48 * 1024 * 1024
        ),
    )(
        live_rows, span_start, query_nope, query_rope, latent, key_rope.T, up_keys, up_values,
        jnp.transpose(out_weight, (0, 2, 1)),
    )


def solution(mesh):
    placed = (
        P("ctx", "hg", None),
        P("ctx", "hg", None),
        P("ctx", None),
        P("ctx", None),
        P(None, "hg", None),
        P(None, "hg", None),
        P("hg", None, "ctx"),
        P("ctx"),
        P(),
    )
    return jax.shard_map(
        per_device, mesh=mesh, in_specs=placed, out_specs=P("hg", "ctx"), check_vma=False
    )
```

```python
import math

import jax
import jax.numpy as jnp
from jax import lax
from jax.experimental import pallas as pl
from jax.experimental.pallas import tpu as pltpu
from jax.sharding import PartitionSpec as P

NEG = -1e30
NCTX, NX, NZ, NHG = 32, 4, 8, 16
TOK, HD, DIM, ROPE, LAT, SLOTS, COLS = 128, 8, 128, 64, 512, 768, 224
PAIRS = HD // 2
FACTOR = 1.0 / math.sqrt(DIM + ROPE)
MESH = pl.DeviceIdType.MESH
F32, BF16 = jnp.float32, jnp.bfloat16
NEAR_FIRST = (1, 7, 2, 6, 3, 5, 4)
FAR_FIRST = (4, 3, 5, 2, 6, 1, 7)


def rows(start, size):
    return pl.ds(pl.multiple_of(start, size), size)


def kernel(
    live_h, span_h, qn_h, qr_h, latent, rope_t, up_k, up_v, weight_t, out,
    live, span, qn, qr, lat_v, rope_v, upk_v, upv_v, wt_v, small, wide, wk, wvt,
    keys, values_t, kr, qa_all, qb_all, q_wide, r_wide, counts,
    o_mine, lse_mine, o_all, lse_all, a_all, part, part_all,
    load_sem, q_send, qz_recv, qx_recv, n_send, nz_recv, nx_recv,
    o_send, o_recv, lse_send, lse_recv, a_send, az_recv, ax_recv, ab_recv, p_send, p_recv,
):
    c, g = lax.axis_index("ctx"), lax.axis_index("hg")
    z, x = lax.rem(c, NZ), lax.div(c, NZ)
    column = x * NZ

    def z_peer(k):
        return column + lax.rem(z + k, NZ)

    def x_peer(k):
        return lax.rem(c + NZ * k, NCTX)

    def h_peer(k):
        return lax.rem(g + k, NHG)

    def send(src, dst, send_sem, recv_sem, ctx, hg):
        pltpu.make_async_remote_copy(
            src_ref=src, dst_ref=dst, send_sem=send_sem, recv_sem=recv_sem,
            device_id=(ctx, hg), device_id_type=MESH,
        ).start()

    def drain(ref, sem):
        pltpu.make_async_copy(ref, ref, sem).wait()

    barrier = pltpu.get_barrier_semaphore()
    for k in range(1, NZ):
        pl.semaphore_signal(barrier, inc=1, device_id=(z_peer(k), g), device_id_type=MESH)
    for k in range(1, NX):
        pl.semaphore_signal(barrier, inc=1, device_id=(x_peer(k), g), device_id_type=MESH)
    for k in range(1, NHG):
        pl.semaphore_signal(barrier, inc=1, device_id=(c, h_peer(k)), device_id_type=MESH)

    loads = [
        pltpu.make_async_copy(src, dst, load_sem.at[i])
        for i, (src, dst) in enumerate(
            (
                (live_h, live), (span_h, span), (qn_h, qn), (qr_h, qr),
                (up_k, upk_v), (latent, lat_v), (up_v, upv_v), (rope_t, rope_v), (weight_t, wt_v),
            )
        )
    ]
    for load in loads:
        load.start()
    for load in loads[:4]:
        load.wait()

    count = live[0]
    small[0] = qn[...].astype(F32).reshape(4 * HD, DIM)
    rope = qr[...].astype(F32).reshape(4 * HD, ROPE)
    small[1] = jnp.concatenate([rope, rope], axis=1)
    even, odd = pl.ds(0, 16, stride=2), pl.ds(1, 16, stride=2)
    lane = lax.broadcasted_iota(jnp.int32, (16, DIM), 1)
    mine16, mine32 = rows(c * 16, 16), rows(c * 32, 32)
    both = jnp.where(lane < ROPE, small[1, even, :], small[1, odd, :])
    qa_all[mine32, :] = jnp.concatenate([small[0, even, :], both], axis=0).astype(BF16)
    qb_all[mine16, :] = small[0, odd, :].astype(BF16)
    counts[c] = jnp.zeros((1, DIM), F32) + count.astype(F32)

    pl.semaphore_wait(barrier, (NZ - 1) + (NX - 1) + (NHG - 1))

    q_parts = ((qa_all, 32), (qb_all, 16))
    for i, (ref, size) in enumerate(q_parts):
        block = ref.at[rows(c * size, size)]
        for k in FAR_FIRST:
            send(block, block, q_send.at[i], qz_recv.at[i, k], z_peer(k), g)
            if i == 0:
                send(counts.at[c], counts.at[c], n_send, nz_recv, z_peer(k), g)
        for j in (2, 1, 3):
            send(block, block, q_send.at[i], qx_recv.at[i], x_peer(j), g)

    loads[4].wait()
    wide[...] = upk_v[...].astype(F32).reshape(LAT * HD, DIM)
    for h in range(HD):
        wk[:, h * DIM : (h + 1) * DIM] = wide[pl.ds(h, LAT, stride=HD), :].astype(BF16)
    loads[5].wait()
    for h in range(0, HD, 2):
        two = jnp.dot(
            lat_v[...], wk[:, h * DIM : (h + 2) * DIM], preferred_element_type=F32
        ).astype(BF16)
        keys[h] = two[:, 0:DIM]
        keys[h + 1] = two[:, DIM:]

    loads[6].wait()
    wide[...] = upv_v[...].astype(F32).reshape(LAT * HD, DIM)
    for h in range(HD):
        wvt[h * DIM : (h + 1) * DIM, :] = wide[pl.ds(h, LAT, stride=HD), :].T.astype(BF16)
    for n in range(0, SLOTS, 256):
        values_t[:, n : n + 256] = lax.dot_general(
            wvt[...], lat_v[n : n + 256, :], (((1,), (1,)), ((), ())),
            preferred_element_type=F32,
        ).astype(BF16)
    loads[7].wait()
    rope = rope_v[...].astype(F32)
    blank = jnp.zeros((DIM - ROPE, SLOTS), F32)
    kr[0] = jnp.concatenate([rope, blank], axis=0).T.astype(BF16)
    kr[1] = jnp.concatenate([blank, rope], axis=0).T.astype(BF16)

    for i, (ref, size) in enumerate(q_parts):
        for k in NEAR_FIRST:
            block = ref.at[rows(z_peer(k) * size, size)]
            drain(block, qz_recv.at[i, NZ - k])
            for j in (2, 1, 3):
                send(block, block, q_send.at[i], qx_recv.at[i], x_peer(j), g)
        if i == 0:
            drain(counts.at[pl.ds(0, NZ - 1)], nz_recv)
            some = counts.at[rows(column, NZ)]
            for j in (2, 1, 3):
                send(some, some, n_send, nx_recv, x_peer(j), g)

    drain(counts.at[pl.ds(0, 24)], nx_recv)
    shard = lax.broadcasted_iota(jnp.int32, (NCTX, DIM), 0)
    before = jnp.where(shard < c, counts[:, 0, :], 0.0)
    offset = jnp.sum(before, axis=0, keepdims=True).astype(jnp.int32)
    token = lax.broadcasted_iota(jnp.int32, (1, TOK), 1)
    limit = jnp.minimum(token + (span[0] + 1) - offset, count)
    slot = lax.broadcasted_iota(jnp.int32, (SLOTS, TOK), 0)

    for i, (ref, size) in enumerate(q_parts):
        drain(ref.at[pl.ds(0, 24 * size)], qx_recv.at[i])
        got = ref[...].astype(F32).reshape(NCTX, size, DIM)
        q_wide[...] = got[:, 0:16].reshape(NCTX * 16, DIM)
        if i == 0:
            r_wide[...] = got[:, 16:32].reshape(NCTX * 16, DIM)
        for t in range(PAIRS):
            p = lax.rem(x + 1 + t, NX)
            h = 2 * p + i
            mine = pl.ds(p, TOK, stride=PAIRS)
            q = jnp.concatenate(
                [q_wide[mine, :].astype(BF16), r_wide[mine, :].astype(BF16)], axis=1
            )
            k_cat = jnp.concatenate([keys[h], kr[i]], axis=1)
            scores = lax.dot_general(
                k_cat, q, (((1,), (1,)), ((), ())), preferred_element_type=F32
            )
            scores = jnp.where(slot < limit, scores, NEG)
            top = jnp.max(scores, axis=0, keepdims=True)
            weights = jnp.exp((scores - top) * FACTOR)
            total = jnp.sum(weights, axis=0, keepdims=True)
            lse_mine[i, p] = top * FACTOR + jnp.log(total)
            summed = jnp.dot(
                values_t[rows(h * DIM, DIM), :], weights.astype(BF16), preferred_element_type=F32
            )
            o_mine[i, rows(p * DIM, DIM), :] = (summed / total).astype(BF16)
            for j in (4, 3, 5, 2, 6, 1, 7, 0):
                if t == PAIRS - 1 and j == 0:
                    continue
                dst = p * NZ + lax.rem(z + j, NZ)
                place = lax.rem(c - dst + NCTX, NCTX)
                send(
                    lse_mine.at[i, p], lse_all.at[i, place], lse_send.at[i], lse_recv.at[i], dst, g
                )
                send(
                    o_mine.at[i, rows(dst * 16, 16)], o_all.at[i, rows(place * 16, 16)],
                    o_send.at[i], o_recv.at[i], dst, g,
                )

    for i in range(2):
        o_all[i, 0:16, :] = o_mine[i, mine16, :]
        lse_all[i, 0] = lse_mine[i, x]
        drain(lse_all.at[i, pl.ds(1, NCTX - 1)], lse_recv.at[i])
        lse = lse_all[i, :, 0, :]
        share = jnp.exp(lse - jnp.max(lse, axis=0, keepdims=True))
        share = share / jnp.sum(share, axis=0, keepdims=True)
        drain(o_all.at[i, pl.ds(16, (NCTX - 1) * 16)], o_recv.at[i])
        joined = jnp.zeros((16, TOK), F32)
        for s in range(NCTX):
            joined = joined + o_all[i, s * 16 : (s + 1) * 16, :].astype(F32) * share[s : s + 1, :]
        a_all[i, mine16, :] = joined.astype(BF16)
        block = a_all.at[i, mine16]
        if i == 0:
            for k in FAR_FIRST:
                send(block, block, a_send.at[i], az_recv.at[k], z_peer(k), g)
            for j in (2, 1, 3):
                send(block, block, a_send.at[i], ax_recv, x_peer(j), g)
        else:
            for k in FAR_FIRST + (0,):
                for j in (2, 1, 3, 0):
                    if k or j:
                        dst = lax.rem(z_peer(k) + NZ * j, NCTX)
                        send(block, block, a_send.at[i], ab_recv, dst, g)
    for k in NEAR_FIRST:
        block = a_all.at[0, rows(z_peer(k) * 16, 16)]
        drain(block, az_recv.at[NZ - k])
        for j in (2, 1, 3):
            send(block, block, a_send.at[0], ax_recv, x_peer(j), g)

    loads[8].wait()
    w = [jnp.concatenate([wt_v[2 * p + i] for p in range(PAIRS)], axis=1) for i in range(2)]
    drain(a_all.at[0, pl.ds(0, 24 * 16)], ax_recv)
    mixed_t = jnp.dot(w[0], a_all[0], preferred_element_type=F32)
    drain(a_all.at[1, pl.ds(0, (NCTX - 1) * 16)], ab_recv)
    mixed_t = mixed_t + jnp.dot(w[1], a_all[1], preferred_element_type=F32)
    mixed_t = jnp.concatenate([mixed_t, jnp.zeros((256 - COLS, TOK), F32)], axis=0)
    left = mixed_t[0:128].T.reshape(NHG, 8, 128)
    right = mixed_t[128:].T.reshape(NHG, 8, 128)
    part[...] = jnp.concatenate([left, right], axis=1).astype(BF16).reshape(NHG * 16, 128)
    for k in (8, 9, 7, 10, 6, 11, 5, 12, 4, 13, 3, 14, 2, 15, 1):
        send(
            part.at[rows(h_peer(k) * 16, 16)], part_all.at[pl.ds((NHG - k) * 16, 16)],
            p_send, p_recv, c, h_peer(k),
        )
    acc = part[rows(g * 16, 16), :].astype(F32)
    drain(part_all.at[pl.ds(16, (NHG - 1) * 16)], p_recv)
    for k in range(1, NHG):
        acc = acc + part_all[k * 16 : (k + 1) * 16, :].astype(F32)
    out[...] = jnp.concatenate([acc[0:8], acc[8:16, 0 : COLS - 128]], axis=1).astype(BF16)

    for i, (ref, size) in enumerate(q_parts):
        drain(ref.at[pl.ds(0, 31 * size)], q_send.at[i])
        drain(o_all.at[i, pl.ds(16, (NCTX - 1) * 16)], o_send.at[i])
        drain(lse_all.at[i, pl.ds(1, NCTX - 1)], lse_send.at[i])
        drain(a_all.at[i, pl.ds(0, (NCTX - 1) * 16)], a_send.at[i])
    drain(counts.at[pl.ds(0, 31)], n_send)
    drain(part_all.at[pl.ds(16, (NHG - 1) * 16)], p_send)


def per_device(
    query_nope, query_rope, latent, key_rope, up_keys, up_values, out_weight, live_rows, span_start
):
    hbm = pl.BlockSpec(memory_space=pltpu.HBM)
    dma = pltpu.SemaphoreType.DMA
    call = pl.pallas_call(
        kernel,
        out_shape=jax.ShapeDtypeStruct((TOK // NHG, COLS), BF16),
        in_specs=[hbm] * 9,
        out_specs=pl.BlockSpec(memory_space=pltpu.VMEM),
        scratch_shapes=[
            pltpu.SMEM((1,), jnp.int32),
            pltpu.SMEM((1,), jnp.int32),
            pltpu.VMEM((4, HD, DIM), BF16),
            pltpu.VMEM((4, HD, ROPE), BF16),
            pltpu.VMEM((SLOTS, LAT), BF16),
            pltpu.VMEM((ROPE, SLOTS), BF16),
            pltpu.VMEM((LAT, HD, DIM), BF16),
            pltpu.VMEM((LAT, HD, DIM), BF16),
            pltpu.VMEM((HD, COLS, DIM), BF16),
            pltpu.VMEM((2, 4 * HD, DIM), F32),
            pltpu.VMEM((LAT * HD, DIM), F32),
            pltpu.VMEM((LAT, HD * DIM), BF16),
            pltpu.VMEM((HD * DIM, LAT), BF16),
            pltpu.VMEM((HD, SLOTS, DIM), BF16),
            pltpu.VMEM((HD * DIM, SLOTS), BF16),
            pltpu.VMEM((2, SLOTS, DIM), BF16),
            pltpu.VMEM((NCTX * 32, DIM), BF16),
            pltpu.VMEM((NCTX * 16, DIM), BF16),
            pltpu.VMEM((NCTX * 16, DIM), F32),
            pltpu.VMEM((NCTX * 16, DIM), F32),
            pltpu.VMEM((NCTX, 1, DIM), F32),
            pltpu.VMEM((2, PAIRS * DIM, TOK), BF16),
            pltpu.VMEM((2, PAIRS, 1, TOK), F32),
            pltpu.VMEM((2, NCTX * 16, TOK), BF16),
            pltpu.VMEM((2, NCTX, 1, TOK), F32),
            pltpu.VMEM((2, PAIRS * DIM, TOK), BF16),
            pltpu.VMEM((NHG * 16, 128), BF16),
            pltpu.VMEM((NHG * 16, 128), BF16),
            dma((9,)), dma((2,)), dma((2, NZ)), dma((2,)), dma, dma, dma,
            dma((2,)), dma((2,)), dma((2,)), dma((2,)), dma((2,)), dma((NZ,)), dma, dma, dma, dma,
        ],
        compiler_params=pltpu.CompilerParams(
            collective_id=0, has_side_effects=True, vmem_limit_bytes=48 * 1024 * 1024
        ),
    )
    large = (
        query_nope, query_rope, latent, key_rope.T, up_keys, up_values,
        jnp.transpose(out_weight, (0, 2, 1)),
    )
    return call(
        live_rows, span_start, *[pltpu.with_memory_space_constraint(a, pltpu.HBM) for a in large]
    )


def solution(mesh):
    placed = (
        P("ctx", "hg", None),
        P("ctx", "hg", None),
        P("ctx", None),
        P("ctx", None),
        P(None, "hg", None),
        P(None, "hg", None),
        P("hg", None, "ctx"),
        P("ctx"),
        P(),
    )
    return jax.shard_map(
        per_device, mesh=mesh, in_specs=placed, out_specs=P("hg", "ctx"), check_vma=False
    )
```

```python
import math

import jax
import jax.numpy as jnp
from jax import lax
from jax.experimental import pallas as pl
from jax.experimental.pallas import tpu as pltpu
from jax.sharding import PartitionSpec as P

NEG = -1e30
NCTX, NX, NZ, NHG = 32, 4, 8, 16
TOK, HD, DIM, ROPE, LAT, SLOTS, COLS = 128, 8, 128, 64, 512, 768, 224
PAIRS = HD // 2
LOG2E = math.log2(math.e)
FACTOR2 = LOG2E / math.sqrt(DIM + ROPE)
MESH = pl.DeviceIdType.MESH
F32, BF16 = jnp.float32, jnp.bfloat16
NEAR_FIRST = (1, 7, 2, 6, 3, 5, 4)
FAR_FIRST = (4, 3, 5, 2, 6, 1, 7)
HOT = 2
OWNER_ORDER = ((4, 2, 6, 0), (3, 5, 1, 7))
PASS_ORDER = (0, 2, 4, 6, 1, 3, 5, 7)


def rows(start, size):
    return pl.ds(pl.multiple_of(start, size), size)


def kernel(
    live_h, span_h, qn_h, qr_h, latent, rope_t, up_k, up_v, weight_t, out,
    live, span, qn, qr, lat_v, rope_v, upk_v, upv_v, wt_v, small, wide, wk, wvt,
    keys, values_t, kr, qa_all, qb_all, q_wide, r_wide, counts,
    o_mine, lse_mine, o_all, lse_all, a_all, part, part_all,
    load_sem, q_send, qz_recv, qx_recv, n_send, nz_recv, nx_recv,
    o_send, o_recv, lse_send, lse_recv, a_send, az_recv, ax_recv, p_send, p_recv,
):
    c, g = lax.axis_index("ctx"), lax.axis_index("hg")
    z, x = lax.rem(c, NZ), lax.div(c, NZ)
    column = x * NZ

    def z_peer(k):
        return column + lax.rem(z + k, NZ)

    def x_peer(k):
        return lax.rem(c + NZ * k, NCTX)

    def zx_peer(k, j):
        return lax.rem(z_peer(k) + NZ * j, NCTX)

    def h_peer(k):
        return lax.rem(g + k, NHG)

    def send(src, dst, send_sem, recv_sem, ctx, hg):
        pltpu.make_async_remote_copy(
            src_ref=src, dst_ref=dst, send_sem=send_sem, recv_sem=recv_sem,
            device_id=(ctx, hg), device_id_type=MESH,
        ).start()

    def drain(ref, sem):
        pltpu.make_async_copy(ref, ref, sem).wait()

    barrier = pltpu.get_barrier_semaphore()
    for k in FAR_FIRST:
        pl.semaphore_signal(barrier, inc=1, device_id=(z_peer(k), g), device_id_type=MESH)
    for k in range(1, NX):
        pl.semaphore_signal(barrier, inc=1, device_id=(x_peer(k), g), device_id_type=MESH)
    for k in range(1, NHG):
        pl.semaphore_signal(barrier, inc=1, device_id=(c, h_peer(k)), device_id_type=MESH)

    loads = [
        pltpu.make_async_copy(src, dst, load_sem.at[i])
        for i, (src, dst) in enumerate(
            (
                (live_h, live), (span_h, span), (qn_h, qn), (qr_h, qr),
                (up_k, upk_v), (latent, lat_v), (up_v, upv_v), (rope_t, rope_v), (weight_t, wt_v),
            )
        )
    ]
    for load in loads:
        load.start()
    for load in loads[:4]:
        load.wait()

    count = live[0]
    small[0] = qn[...].astype(F32).reshape(4 * HD, DIM)
    rope = qr[...].astype(F32).reshape(4 * HD, ROPE)
    small[1] = jnp.concatenate([rope, rope], axis=1)
    even, odd = pl.ds(0, 16, stride=2), pl.ds(1, 16, stride=2)
    lane = lax.broadcasted_iota(jnp.int32, (16, DIM), 1)
    mine16, mine32 = rows(c * 16, 16), rows(c * 32, 32)
    both = jnp.where(lane < ROPE, small[1, even, :], small[1, odd, :])
    qa_all[mine32, :] = jnp.concatenate([small[0, even, :], both], axis=0).astype(BF16)
    qb_all[mine16, :] = small[0, odd, :].astype(BF16)
    counts[c] = jnp.zeros((1, DIM), F32) + count.astype(F32)

    pl.semaphore_wait(barrier, (NZ - 1) + (NX - 1) + (NHG - 1))

    q_parts = ((qa_all, 32), (qb_all, 16))

    def to_x(block, send_sem, x_sem):
        for j in (2, 1, 3):
            send(block, block, send_sem, x_sem, x_peer(j), g)

    for i, (ref, size) in enumerate(q_parts):
        block = ref.at[rows(c * size, size)]
        for k in FAR_FIRST:
            send(block, block, q_send.at[i], qz_recv.at[i, k], z_peer(k), g)
        to_x(block, q_send.at[i], qx_recv.at[i])
        if i == 0:
            for k in FAR_FIRST:
                send(counts.at[c], counts.at[c], n_send, nz_recv, z_peer(k), g)

    loads[4].wait()
    wide[...] = upk_v[...].astype(F32).reshape(LAT * HD, DIM)
    for h in range(HD):
        wk[:, h * DIM : (h + 1) * DIM] = wide[pl.ds(h, LAT, stride=HD), :].astype(BF16)
    loads[5].wait()
    for h in range(0, HD, 2):
        two = jnp.dot(
            lat_v[...], wk[:, h * DIM : (h + 2) * DIM], preferred_element_type=F32
        ).astype(BF16)
        keys[h] = two[:, 0:DIM]
        keys[h + 1] = two[:, DIM:]

    loads[6].wait()
    wide[...] = upv_v[...].astype(F32).reshape(LAT * HD, DIM)
    for h in range(HD):
        wvt[h * DIM : (h + 1) * DIM, :] = wide[pl.ds(h, LAT, stride=HD), :].T.astype(BF16)
    for n in range(0, SLOTS, 256):
        values_t[:, n : n + 256] = lax.dot_general(
            wvt[...], lat_v[n : n + 256, :], (((1,), (1,)), ((), ())),
            preferred_element_type=F32,
        ).astype(BF16)
    loads[7].wait()
    rope = rope_v[...].astype(F32)
    blank = jnp.zeros((DIM - ROPE, SLOTS), F32)
    kr[0] = jnp.concatenate([rope, blank], axis=0).T.astype(BF16)
    kr[1] = jnp.concatenate([blank, rope], axis=0).T.astype(BF16)

    for i, (ref, size) in enumerate(q_parts):
        for k in NEAR_FIRST:
            block = ref.at[rows(z_peer(k) * size, size)]
            drain(block, qz_recv.at[i, NZ - k])
            to_x(block, q_send.at[i], qx_recv.at[i])
        if i == 0:
            drain(counts.at[pl.ds(0, NZ - 1)], nz_recv)
            to_x(counts.at[rows(column, NZ)], n_send, nx_recv)

    drain(counts.at[pl.ds(0, 24)], nx_recv)
    shard = lax.broadcasted_iota(jnp.int32, (NCTX, DIM), 0)
    before = jnp.where(shard < c, counts[:, 0, :], 0.0)
    offset = jnp.sum(before, axis=0, keepdims=True).astype(jnp.int32)
    token = lax.broadcasted_iota(jnp.int32, (1, TOK), 1)
    limit = jnp.minimum(token + (span[0] + 1) - offset, count)
    slot = lax.broadcasted_iota(jnp.int32, (SLOTS, TOK), 0)

    def scores_of(i, t):
        p = lax.rem(x + 1 + t, NX)
        mine = pl.ds(p, TOK, stride=PAIRS)
        q = jnp.concatenate([q_wide[mine, :].astype(BF16), r_wide[mine, :].astype(BF16)], axis=1)
        k_cat = jnp.concatenate([keys[2 * p + i], kr[i]], axis=1)
        return lax.dot_general(k_cat, q, (((1,), (1,)), ((), ())), preferred_element_type=F32)

    def weights_of(i, t, scores):
        scores = jnp.where(slot < limit, scores, NEG)
        top = jnp.max(scores, axis=0, keepdims=True)
        weights = jnp.exp2((scores - top) * FACTOR2)
        total = jnp.sum(weights, axis=0, keepdims=True)
        lse_mine[i, lax.rem(x + 1 + t, NX)] = top * FACTOR2 + jnp.log(total) * LOG2E
        return weights.astype(BF16), 1.0 / total

    def values_of(i, t, weights, scale):
        p = lax.rem(x + 1 + t, NX)
        summed = jnp.dot(
            values_t[rows((2 * p + i) * DIM, DIM), :], weights, preferred_element_type=F32
        )
        o_mine[i, rows(p * DIM, DIM), :] = (summed * scale).astype(BF16)

    def give_out(i, t):
        p = lax.rem(x + 1 + t, NX)
        for zz in OWNER_ORDER[i]:
            dst = p * NZ + zz
            place = lax.rem(c - dst + NCTX, NCTX)
            mine = rows((p * 4 + zz // 2) * 32, 32)

            def go():
                send(lse_mine.at[i, p], lse_all.at[place], lse_send, lse_recv, dst, g)
                send(
                    o_mine.at[i, mine], o_all.at[rows(place * 32, 32)], o_send, o_recv, dst, g
                )

            if t < PAIRS - 1:
                go()
            else:
                pl.when(zz != z)(go)

    for i, (ref, size) in enumerate(q_parts):
        drain(ref.at[pl.ds(0, 24 * size)], qx_recv.at[i])
        got = ref[...].astype(F32).reshape(NCTX, size, DIM)
        q_wide[...] = got[:, 0:16].reshape(NCTX * 16, DIM)
        if i == 0:
            r_wide[...] = got[:, 16:32].reshape(NCTX * 16, DIM)
        coming = scores_of(i, 0)
        for t in range(PAIRS):
            scores = coming
            if t < PAIRS - 1:
                coming = scores_of(i, t + 1)
            values_of(i, t, *weights_of(i, t, scores))
            give_out(i, t)

    group, place = lax.rem(z, 2), x * 4 + lax.div(z, 2)
    own = rows(place * 32, 32)
    o_all[0:32, :] = o_mine[group, own, :]
    lse_all[0] = lse_mine[group, x]
    drain(lse_all.at[pl.ds(1, NCTX - 1)], lse_recv)
    lse = lse_all[:, 0, :]
    share = jnp.exp2(lse - jnp.max(lse, axis=0, keepdims=True))
    share = share / jnp.sum(share, axis=0, keepdims=True)
    drain(o_all.at[pl.ds(32, (NCTX - 1) * 32)], o_recv)
    joined = jnp.zeros((32, TOK), F32)
    for s in range(NCTX):
        joined = joined + o_all[s * 32 : (s + 1) * 32, :].astype(F32) * share[s : s + 1, :]
    a_all[group, own, :] = joined.astype(BF16)
    block = a_all.at[group, own]
    for zz in range(HOT):
        @pl.when(z != zz)
        def _():
            send(block, block, a_send, az_recv.at[z], column + zz, g)

        for j in (2, 1, 3):
            dst = lax.rem(column + NZ * j, NCTX) + zz
            send(block, block, a_send, ax_recv.at[group], dst, g)
    for k in FAR_FIRST:
        @pl.when(lax.rem(z + k, NZ) >= HOT)
        def _():
            send(block, block, a_send, az_recv.at[z], z_peer(k), g)

    @pl.when(z >= HOT)
    def _():
        to_x(block, a_send, ax_recv.at[group])

    def pass_on(zz):
        @pl.when(zz != z)
        def _():
            block = a_all.at[zz % 2, rows((x * 4 + zz // 2) * 32, 32)]
            drain(block, az_recv.at[zz])

            @pl.when(z >= HOT)
            def _():
                to_x(block, a_send, ax_recv.at[zz % 2])

    loads[8].wait()
    w = [jnp.concatenate([wt_v[2 * p + i] for p in range(PAIRS)], axis=1) for i in range(2)]
    for zz in PASS_ORDER:
        pass_on(zz)
    drain(a_all.at[0, pl.ds(0, 12 * 32)], ax_recv.at[0])
    mixed_t = jnp.dot(w[0], a_all[0], preferred_element_type=F32)
    drain(a_all.at[1, pl.ds(0, 12 * 32)], ax_recv.at[1])
    mixed_t = mixed_t + jnp.dot(w[1], a_all[1], preferred_element_type=F32)
    mixed_t = jnp.concatenate([mixed_t, jnp.zeros((256 - COLS, TOK), F32)], axis=0)
    left = mixed_t[0:128].T.reshape(NHG, 8, 128)
    right = mixed_t[128:].T.reshape(NHG, 8, 128)
    part[...] = jnp.concatenate([left, right], axis=1).astype(BF16).reshape(NHG * 16, 128)
    for dst in (0, 1, 8, 9, 6, 7, 10, 11, 4, 5, 12, 13, 2, 3, 14, 15):
        @pl.when(g != dst)
        def _():
            place = lax.rem(g - dst + NHG, NHG)
            send(
                part.at[dst * 16 : (dst + 1) * 16], part_all.at[rows(place * 16, 16)],
                p_send, p_recv, c, dst,
            )

    acc = part[rows(g * 16, 16), :].astype(F32)
    drain(part_all.at[pl.ds(16, (NHG - 1) * 16)], p_recv)
    for k in range(1, NHG):
        acc = acc + part_all[k * 16 : (k + 1) * 16, :].astype(F32)
    out[...] = jnp.concatenate([acc[0:8], acc[8:16, 0 : COLS - 128]], axis=1).astype(BF16)

    for i, (ref, size) in enumerate(q_parts):
        drain(ref.at[pl.ds(0, 31 * size)], q_send.at[i])
    drain(o_all.at[pl.ds(32, (NCTX - 1) * 32)], o_send)
    drain(lse_all.at[pl.ds(1, NCTX - 1)], lse_send)
    drain(o_all.at[pl.ds(0, (NZ - 1 + 3 * HOT) * 32)], a_send)

    @pl.when(z >= HOT)
    def _():
        drain(o_all.at[pl.ds(0, 24 * 32)], a_send)

    drain(counts.at[pl.ds(0, 31)], n_send)
    drain(part_all.at[pl.ds(16, (NHG - 1) * 16)], p_send)


def per_device(
    query_nope, query_rope, latent, key_rope, up_keys, up_values, out_weight, live_rows, span_start
):
    hbm = pl.BlockSpec(memory_space=pltpu.HBM)
    dma = pltpu.SemaphoreType.DMA
    call = pl.pallas_call(
        kernel,
        out_shape=jax.ShapeDtypeStruct((TOK // NHG, COLS), BF16),
        in_specs=[hbm] * 9,
        out_specs=pl.BlockSpec(memory_space=pltpu.VMEM),
        scratch_shapes=[
            pltpu.SMEM((1,), jnp.int32),
            pltpu.SMEM((1,), jnp.int32),
            pltpu.VMEM((4, HD, DIM), BF16),
            pltpu.VMEM((4, HD, ROPE), BF16),
            pltpu.VMEM((SLOTS, LAT), BF16),
            pltpu.VMEM((ROPE, SLOTS), BF16),
            pltpu.VMEM((LAT, HD, DIM), BF16),
            pltpu.VMEM((LAT, HD, DIM), BF16),
            pltpu.VMEM((HD, COLS, DIM), BF16),
            pltpu.VMEM((2, 4 * HD, DIM), F32),
            pltpu.VMEM((LAT * HD, DIM), F32),
            pltpu.VMEM((LAT, HD * DIM), BF16),
            pltpu.VMEM((HD * DIM, LAT), BF16),
            pltpu.VMEM((HD, SLOTS, DIM), BF16),
            pltpu.VMEM((HD * DIM, SLOTS), BF16),
            pltpu.VMEM((2, SLOTS, DIM), BF16),
            pltpu.VMEM((NCTX * 32, DIM), BF16),
            pltpu.VMEM((NCTX * 16, DIM), BF16),
            pltpu.VMEM((NCTX * 16, DIM), F32),
            pltpu.VMEM((NCTX * 16, DIM), F32),
            pltpu.VMEM((NCTX, 1, DIM), F32),
            pltpu.VMEM((2, PAIRS * DIM, TOK), BF16),
            pltpu.VMEM((2, PAIRS, 1, TOK), F32),
            pltpu.VMEM((NCTX * 32, TOK), BF16),
            pltpu.VMEM((NCTX, 1, TOK), F32),
            pltpu.VMEM((2, PAIRS * DIM, TOK), BF16),
            pltpu.VMEM((NHG * 16, 128), BF16),
            pltpu.VMEM((NHG * 16, 128), BF16),
            dma((9,)), dma((2,)), dma((2, NZ)), dma((2,)), dma, dma, dma,
            dma, dma, dma, dma, dma, dma((NZ,)), dma((2,)), dma, dma,
        ],
        compiler_params=pltpu.CompilerParams(
            collective_id=0, has_side_effects=True, vmem_limit_bytes=48 * 1024 * 1024
        ),
    )
    large = (
        query_nope, query_rope, latent, key_rope.T, up_keys, up_values,
        jnp.transpose(out_weight, (0, 2, 1)),
    )
    return call(
        live_rows, span_start, *[pltpu.with_memory_space_constraint(a, pltpu.HBM) for a in large]
    )


def solution(mesh):
    placed = (
        P("ctx", "hg", None),
        P("ctx", "hg", None),
        P("ctx", None),
        P("ctx", None),
        P(None, "hg", None),
        P(None, "hg", None),
        P("hg", None, "ctx"),
        P("ctx"),
        P(),
    )
    return jax.shard_map(
        per_device, mesh=mesh, in_specs=placed, out_specs=P("hg", "ctx"), check_vma=False
    )
```

```python
import math

import jax
import jax.numpy as jnp
from jax import lax
from jax.experimental import pallas as pl
from jax.experimental.pallas import tpu as pltpu
from jax.sharding import PartitionSpec as P

NEG = -1e30
NCTX, NX, NZ, NHG = 32, 4, 8, 16
TOK, HD, DIM, ROPE, LAT, SLOTS, COLS = 128, 8, 128, 64, 512, 768, 224
PAIRS = HD // 2
LOG2E = math.log2(math.e)
FACTOR2 = LOG2E / math.sqrt(DIM + ROPE)
MESH = pl.DeviceIdType.MESH
F32, BF16 = jnp.float32, jnp.bfloat16
NEAR_FIRST = (1, 7, 2, 6, 3, 5, 4)
FAR_FIRST = (4, 3, 5, 2, 6, 1, 7)
HOT = 2
VIA_X = (1, 7, 2, 6)
OWNER_ORDER = ((4, 2, 6, 0), (3, 5, 1, 7))
PASS_ORDER = (0, 2, 4, 6, 1, 3, 5, 7)


def rows(start, size):
    return pl.ds(pl.multiple_of(start, size), size)


def kernel(
    live_h, span_h, qn_h, qr_h, latent, rope_t, up_k, up_v, weight_t, out,
    live, span, qn, qr, lat_v, rope_v, upk_v, upv_v, wt_v, small, wide, wk, wvt,
    keys, values_t, kr, qa_all, qb_all, q_wide, r_wide, counts,
    o_mine, lse_mine, o_all, lse_all, a_all, part, part_all,
    load_sem, q_send, qz_recv, qx_recv, q2_recv, n_send, nz_recv, nx_recv,
    o_send, o_recv, lse_send, lse_recv, a_send, az_recv, ax_recv, p_send, p_recv,
):
    c, g = lax.axis_index("ctx"), lax.axis_index("hg")
    z, x = lax.rem(c, NZ), lax.div(c, NZ)
    column = x * NZ

    def z_peer(k):
        return column + lax.rem(z + k, NZ)

    def x_peer(k):
        return lax.rem(c + NZ * k, NCTX)

    def zx_peer(k, j):
        return lax.rem(z_peer(k) + NZ * j, NCTX)

    def h_peer(k):
        return lax.rem(g + k, NHG)

    def send(src, dst, send_sem, recv_sem, ctx, hg):
        pltpu.make_async_remote_copy(
            src_ref=src, dst_ref=dst, send_sem=send_sem, recv_sem=recv_sem,
            device_id=(ctx, hg), device_id_type=MESH,
        ).start()

    def drain(ref, sem):
        pltpu.make_async_copy(ref, ref, sem).wait()

    barrier = pltpu.get_barrier_semaphore()
    for k in FAR_FIRST:
        pl.semaphore_signal(barrier, inc=1, device_id=(z_peer(k), g), device_id_type=MESH)
    for k in range(1, NX):
        pl.semaphore_signal(barrier, inc=1, device_id=(x_peer(k), g), device_id_type=MESH)
    for k in range(1, NHG):
        pl.semaphore_signal(barrier, inc=1, device_id=(c, h_peer(k)), device_id_type=MESH)

    loads = [
        pltpu.make_async_copy(src, dst, load_sem.at[i])
        for i, (src, dst) in enumerate(
            (
                (live_h, live), (span_h, span), (qn_h, qn), (qr_h, qr),
                (up_k, upk_v), (latent, lat_v), (up_v, upv_v), (rope_t, rope_v), (weight_t, wt_v),
            )
        )
    ]
    for load in loads:
        load.start()
    for load in loads[:4]:
        load.wait()

    count = live[0]
    small[0] = qn[...].astype(F32).reshape(4 * HD, DIM)
    rope = qr[...].astype(F32).reshape(4 * HD, ROPE)
    small[1] = jnp.concatenate([rope, rope], axis=1)
    even, odd = pl.ds(0, 16, stride=2), pl.ds(1, 16, stride=2)
    lane = lax.broadcasted_iota(jnp.int32, (16, DIM), 1)
    mine16, mine32 = rows(c * 16, 16), rows(c * 32, 32)
    both = jnp.where(lane < ROPE, small[1, even, :], small[1, odd, :])
    qa_all[mine32, :] = jnp.concatenate([small[0, even, :], both], axis=0).astype(BF16)
    qb_all[mine16, :] = small[0, odd, :].astype(BF16)
    counts[c] = jnp.zeros((1, DIM), F32) + count.astype(F32)

    pl.semaphore_wait(barrier, (NZ - 1) + (NX - 1) + (NHG - 1))

    q_parts = ((qa_all, 32), (qb_all, 16))

    def to_x(block, send_sem, x_sem):
        for j in (2, 1, 3):
            send(block, block, send_sem, x_sem, x_peer(j), g)

    for i, (ref, size) in enumerate(q_parts):
        block = ref.at[rows(c * size, size)]
        for k in FAR_FIRST:
            send(block, block, q_send.at[i], qz_recv.at[i, k], z_peer(k), g)
        send(block, block, q_send.at[i], q2_recv.at[i], x_peer(2), g)
        for j in (1, 3):
            send(block, block, q_send.at[i], qx_recv.at[i], x_peer(j), g)
        if i == 0:
            for k in FAR_FIRST:
                send(counts.at[c], counts.at[c], n_send, nz_recv, z_peer(k), g)

    loads[4].wait()
    wide[...] = upk_v[...].astype(F32).reshape(LAT * HD, DIM)
    for h in range(HD):
        wk[:, h * DIM : (h + 1) * DIM] = wide[pl.ds(h, LAT, stride=HD), :].astype(BF16)
    loads[5].wait()
    for h in range(0, HD, 2):
        two = jnp.dot(
            lat_v[...], wk[:, h * DIM : (h + 2) * DIM], preferred_element_type=F32
        ).astype(BF16)
        keys[h] = two[:, 0:DIM]
        keys[h + 1] = two[:, DIM:]

    loads[6].wait()
    wide[...] = upv_v[...].astype(F32).reshape(LAT * HD, DIM)
    for h in range(HD):
        wvt[h * DIM : (h + 1) * DIM, :] = wide[pl.ds(h, LAT, stride=HD), :].T.astype(BF16)
    for n in range(0, SLOTS, 256):
        values_t[:, n : n + 256] = lax.dot_general(
            wvt[...], lat_v[n : n + 256, :], (((1,), (1,)), ((), ())),
            preferred_element_type=F32,
        ).astype(BF16)
    loads[7].wait()
    rope = rope_v[...].astype(F32)
    blank = jnp.zeros((DIM - ROPE, SLOTS), F32)
    kr[0] = jnp.concatenate([rope, blank], axis=0).T.astype(BF16)
    kr[1] = jnp.concatenate([blank, rope], axis=0).T.astype(BF16)

    for i, (ref, size) in enumerate(q_parts):
        for k in NEAR_FIRST:
            block = ref.at[rows(z_peer(k) * size, size)]
            drain(block, qz_recv.at[i, NZ - k])
            for j in (1, 3) if NZ - k in VIA_X else (2, 1, 3):
                send(block, block, q_send.at[i], qx_recv.at[i], x_peer(j), g)
            if k == 6:
                across = ref.at[rows(x_peer(2) * size, size)]
                drain(across, q2_recv.at[i])
                for near in VIA_X:
                    send(across, across, q_send.at[i], qx_recv.at[i], z_peer(near), g)
        if i == 0:
            drain(counts.at[pl.ds(0, NZ - 1)], nz_recv)
            to_x(counts.at[rows(column, NZ)], n_send, nx_recv)

    drain(counts.at[pl.ds(0, 24)], nx_recv)
    shard = lax.broadcasted_iota(jnp.int32, (NCTX, DIM), 0)
    before = jnp.where(shard < c, counts[:, 0, :], 0.0)
    offset = jnp.sum(before, axis=0, keepdims=True).astype(jnp.int32)
    token = lax.broadcasted_iota(jnp.int32, (1, TOK), 1)
    limit = jnp.minimum(token + (span[0] + 1) - offset, count)
    slot = lax.broadcasted_iota(jnp.int32, (SLOTS, TOK), 0)

    def scores_of(i, t):
        p = lax.rem(x + 1 + t, NX)
        mine = pl.ds(p, TOK, stride=PAIRS)
        q = jnp.concatenate([q_wide[mine, :].astype(BF16), r_wide[mine, :].astype(BF16)], axis=1)
        k_cat = jnp.concatenate([keys[2 * p + i], kr[i]], axis=1)
        return lax.dot_general(k_cat, q, (((1,), (1,)), ((), ())), preferred_element_type=F32)

    def weights_of(i, t, scores):
        scores = jnp.where(slot < limit, scores, NEG)
        top = jnp.max(scores, axis=0, keepdims=True)
        weights = jnp.exp2((scores - top) * FACTOR2)
        total = jnp.sum(weights, axis=0, keepdims=True)
        lse_mine[i, lax.rem(x + 1 + t, NX)] = top * FACTOR2 + jnp.log(total) * LOG2E
        return weights.astype(BF16), 1.0 / total

    def values_of(i, t, weights, scale):
        p = lax.rem(x + 1 + t, NX)
        summed = jnp.dot(
            values_t[rows((2 * p + i) * DIM, DIM), :], weights, preferred_element_type=F32
        )
        o_mine[i, rows(p * DIM, DIM), :] = (summed * scale).astype(BF16)

    def give_out(i, t):
        p = lax.rem(x + 1 + t, NX)
        for zz in OWNER_ORDER[i]:
            dst = p * NZ + zz
            place = lax.rem(c - dst + NCTX, NCTX)
            mine = rows((p * 4 + zz // 2) * 32, 32)

            def go():
                send(lse_mine.at[i, p], lse_all.at[place], lse_send, lse_recv, dst, g)
                send(
                    o_mine.at[i, mine], o_all.at[rows(place * 32, 32)], o_send, o_recv, dst, g
                )

            if t < PAIRS - 1:
                go()
            else:
                pl.when(zz != z)(go)

    for i, (ref, size) in enumerate(q_parts):
        drain(ref.at[pl.ds(0, 23 * size)], qx_recv.at[i])
        got = ref[...].astype(F32).reshape(NCTX, size, DIM)
        q_wide[...] = got[:, 0:16].reshape(NCTX * 16, DIM)
        if i == 0:
            r_wide[...] = got[:, 16:32].reshape(NCTX * 16, DIM)
        coming = scores_of(i, 0)
        for t in range(PAIRS):
            scores = coming
            if t < PAIRS - 1:
                coming = scores_of(i, t + 1)
            values_of(i, t, *weights_of(i, t, scores))
            give_out(i, t)

    group, place = lax.rem(z, 2), x * 4 + lax.div(z, 2)
    own = rows(place * 32, 32)
    o_all[0:32, :] = o_mine[group, own, :]
    lse_all[0] = lse_mine[group, x]
    drain(lse_all.at[pl.ds(1, NCTX - 1)], lse_recv)
    lse = lse_all[:, 0, :]
    share = jnp.exp2(lse - jnp.max(lse, axis=0, keepdims=True))
    share = share / jnp.sum(share, axis=0, keepdims=True)
    drain(o_all.at[pl.ds(32, (NCTX - 1) * 32)], o_recv)
    joined = jnp.zeros((32, TOK), F32)
    for s in range(NCTX):
        joined = joined + o_all[s * 32 : (s + 1) * 32, :].astype(F32) * share[s : s + 1, :]
    a_all[group, own, :] = joined.astype(BF16)
    block = a_all.at[group, own]
    for zz in range(HOT):
        @pl.when(z != zz)
        def _():
            send(block, block, a_send, az_recv.at[z], column + zz, g)

        for j in (2, 1, 3):
            dst = lax.rem(column + NZ * j, NCTX) + zz
            send(block, block, a_send, ax_recv.at[group], dst, g)
    for k in FAR_FIRST:
        @pl.when(lax.rem(z + k, NZ) >= HOT)
        def _():
            send(block, block, a_send, az_recv.at[z], z_peer(k), g)

    @pl.when(z >= HOT)
    def _():
        to_x(block, a_send, ax_recv.at[group])

    def pass_on(zz):
        @pl.when(zz != z)
        def _():
            block = a_all.at[zz % 2, rows((x * 4 + zz // 2) * 32, 32)]
            drain(block, az_recv.at[zz])

            @pl.when(z >= HOT)
            def _():
                to_x(block, a_send, ax_recv.at[zz % 2])

    loads[8].wait()
    w = [jnp.concatenate([wt_v[2 * p + i] for p in range(PAIRS)], axis=1) for i in range(2)]
    for zz in PASS_ORDER:
        pass_on(zz)
    drain(a_all.at[0, pl.ds(0, 12 * 32)], ax_recv.at[0])
    mixed_t = jnp.dot(w[0], a_all[0], preferred_element_type=F32)
    drain(a_all.at[1, pl.ds(0, 12 * 32)], ax_recv.at[1])
    mixed_t = mixed_t + jnp.dot(w[1], a_all[1], preferred_element_type=F32)
    mixed_t = jnp.concatenate([mixed_t, jnp.zeros((256 - COLS, TOK), F32)], axis=0)
    left = mixed_t[0:128].T.reshape(NHG, 8, 128)
    right = mixed_t[128:].T.reshape(NHG, 8, 128)
    part[...] = jnp.concatenate([left, right], axis=1).astype(BF16).reshape(NHG * 16, 128)
    for dst in (0, 1, 8, 9, 6, 7, 10, 11, 4, 5, 12, 13, 2, 3, 14, 15):
        @pl.when(g != dst)
        def _():
            place = lax.rem(g - dst + NHG, NHG)
            send(
                part.at[dst * 16 : (dst + 1) * 16], part_all.at[rows(place * 16, 16)],
                p_send, p_recv, c, dst,
            )

    acc = part[rows(g * 16, 16), :].astype(F32)
    drain(part_all.at[pl.ds(16, (NHG - 1) * 16)], p_recv)
    for k in range(1, NHG):
        acc = acc + part_all[k * 16 : (k + 1) * 16, :].astype(F32)
    out[...] = jnp.concatenate([acc[0:8], acc[8:16, 0 : COLS - 128]], axis=1).astype(BF16)

    for i, (ref, size) in enumerate(q_parts):
        drain(ref.at[pl.ds(0, 31 * size)], q_send.at[i])
    drain(o_all.at[pl.ds(32, (NCTX - 1) * 32)], o_send)
    drain(lse_all.at[pl.ds(1, NCTX - 1)], lse_send)
    drain(o_all.at[pl.ds(0, (NZ - 1 + 3 * HOT) * 32)], a_send)

    @pl.when(z >= HOT)
    def _():
        drain(o_all.at[pl.ds(0, 24 * 32)], a_send)

    drain(counts.at[pl.ds(0, 31)], n_send)
    drain(part_all.at[pl.ds(16, (NHG - 1) * 16)], p_send)


def per_device(
    query_nope, query_rope, latent, key_rope, up_keys, up_values, out_weight, live_rows, span_start
):
    hbm = pl.BlockSpec(memory_space=pltpu.HBM)
    dma = pltpu.SemaphoreType.DMA
    call = pl.pallas_call(
        kernel,
        out_shape=jax.ShapeDtypeStruct((TOK // NHG, COLS), BF16),
        in_specs=[hbm] * 9,
        out_specs=pl.BlockSpec(memory_space=pltpu.VMEM),
        scratch_shapes=[
            pltpu.SMEM((1,), jnp.int32),
            pltpu.SMEM((1,), jnp.int32),
            pltpu.VMEM((4, HD, DIM), BF16),
            pltpu.VMEM((4, HD, ROPE), BF16),
            pltpu.VMEM((SLOTS, LAT), BF16),
            pltpu.VMEM((ROPE, SLOTS), BF16),
            pltpu.VMEM((LAT, HD, DIM), BF16),
            pltpu.VMEM((LAT, HD, DIM), BF16),
            pltpu.VMEM((HD, COLS, DIM), BF16),
            pltpu.VMEM((2, 4 * HD, DIM), F32),
            pltpu.VMEM((LAT * HD, DIM), F32),
            pltpu.VMEM((LAT, HD * DIM), BF16),
            pltpu.VMEM((HD * DIM, LAT), BF16),
            pltpu.VMEM((HD, SLOTS, DIM), BF16),
            pltpu.VMEM((HD * DIM, SLOTS), BF16),
            pltpu.VMEM((2, SLOTS, DIM), BF16),
            pltpu.VMEM((NCTX * 32, DIM), BF16),
            pltpu.VMEM((NCTX * 16, DIM), BF16),
            pltpu.VMEM((NCTX * 16, DIM), F32),
            pltpu.VMEM((NCTX * 16, DIM), F32),
            pltpu.VMEM((NCTX, 1, DIM), F32),
            pltpu.VMEM((2, PAIRS * DIM, TOK), BF16),
            pltpu.VMEM((2, PAIRS, 1, TOK), F32),
            pltpu.VMEM((NCTX * 32, TOK), BF16),
            pltpu.VMEM((NCTX, 1, TOK), F32),
            pltpu.VMEM((2, PAIRS * DIM, TOK), BF16),
            pltpu.VMEM((NHG * 16, 128), BF16),
            pltpu.VMEM((NHG * 16, 128), BF16),
            dma((9,)), dma((2,)), dma((2, NZ)), dma((2,)), dma((2,)), dma, dma, dma,
            dma, dma, dma, dma, dma, dma((NZ,)), dma((2,)), dma, dma,
        ],
        compiler_params=pltpu.CompilerParams(
            collective_id=0, has_side_effects=True, vmem_limit_bytes=48 * 1024 * 1024
        ),
    )
    large = (
        query_nope, query_rope, latent, key_rope.T, up_keys, up_values,
        jnp.transpose(out_weight, (0, 2, 1)),
    )
    return call(
        live_rows, span_start, *[pltpu.with_memory_space_constraint(a, pltpu.HBM) for a in large]
    )


def solution(mesh):
    placed = (
        P("ctx", "hg", None),
        P("ctx", "hg", None),
        P("ctx", None),
        P("ctx", None),
        P(None, "hg", None),
        P(None, "hg", None),
        P("hg", None, "ctx"),
        P("ctx"),
        P(),
    )
    return jax.shard_map(
        per_device, mesh=mesh, in_specs=placed, out_specs=P("hg", "ctx"), check_vma=False
    )
```

```python
import math

import jax
import jax.numpy as jnp
from jax import lax
from jax.experimental import pallas as pl
from jax.experimental.pallas import tpu as pltpu
from jax.sharding import PartitionSpec as P

NEG = -1e30
NCTX, NX, NZ, NHG = 32, 4, 8, 16
TOK, HD, DIM, ROPE, LAT, SLOTS, COLS = 128, 8, 128, 64, 512, 768, 224
PAIRS = HD // 2
LOG2E = math.log2(math.e)
FACTOR2 = LOG2E / math.sqrt(DIM + ROPE)
MESH = pl.DeviceIdType.MESH
F32, BF16 = jnp.float32, jnp.bfloat16
NEAR_FIRST = (1, 7, 2, 6, 3, 5, 4)
FAR_FIRST = (4, 3, 5, 2, 6, 1, 7)
HOT = 2
VIA_X = (1, 7, 2, 6)
OWNER_ORDER = ((4, 2, 6, 0), (3, 5, 1, 7))
PASS_ORDER = (1, 7, 2, 6, 3, 5, 4)


def rows(start, size):
    return pl.ds(pl.multiple_of(start, size), size)


def kernel(
    live_h, span_h, qn_h, qr_h, latent, rope_t, up_k, up_v, weight_t, out,
    live, span, qn, qr, lat_v, rope_v, upk_v, upv_v, wt_v, small, wide, wk, wvt,
    keys, values_t, kr, qa_all, qb_all, q_wide, r_wide, counts,
    o_mine, lse_mine, o_all, lse_all, a_all, part, part_all,
    load_sem, q_send, qz_recv, qx_recv, q2_recv, n_send, nz_recv, nx_recv,
    o_send, o_recv, lse_send, lse_recv, a_send, az_recv, ax_recv, p_send, p_recv,
):
    c, g = lax.axis_index("ctx"), lax.axis_index("hg")
    z, x = lax.rem(c, NZ), lax.div(c, NZ)
    column = x * NZ

    def z_peer(k):
        return column + lax.rem(z + k, NZ)

    def x_peer(k):
        return lax.rem(c + NZ * k, NCTX)

    def zx_peer(k, j):
        return lax.rem(z_peer(k) + NZ * j, NCTX)

    def h_peer(k):
        return lax.rem(g + k, NHG)

    def send(src, dst, send_sem, recv_sem, ctx, hg):
        pltpu.make_async_remote_copy(
            src_ref=src, dst_ref=dst, send_sem=send_sem, recv_sem=recv_sem,
            device_id=(ctx, hg), device_id_type=MESH,
        ).start()

    def drain(ref, sem):
        pltpu.make_async_copy(ref, ref, sem).wait()

    barrier = pltpu.get_barrier_semaphore()
    for k in FAR_FIRST:
        pl.semaphore_signal(barrier, inc=1, device_id=(z_peer(k), g), device_id_type=MESH)
    for k in range(1, NX):
        pl.semaphore_signal(barrier, inc=1, device_id=(x_peer(k), g), device_id_type=MESH)
    for k in range(1, NHG):
        pl.semaphore_signal(barrier, inc=1, device_id=(c, h_peer(k)), device_id_type=MESH)

    loads = [
        pltpu.make_async_copy(src, dst, load_sem.at[i])
        for i, (src, dst) in enumerate(
            (
                (live_h, live), (span_h, span), (qn_h, qn), (qr_h, qr),
                (up_k, upk_v), (latent, lat_v), (up_v, upv_v), (rope_t, rope_v), (weight_t, wt_v),
            )
        )
    ]
    for load in loads:
        load.start()
    for load in loads[:4]:
        load.wait()

    count = live[0]
    small[0] = qn[...].astype(F32).reshape(4 * HD, DIM)
    rope = qr[...].astype(F32).reshape(4 * HD, ROPE)
    small[1] = jnp.concatenate([rope, rope], axis=1)
    even, odd = pl.ds(0, 16, stride=2), pl.ds(1, 16, stride=2)
    lane = lax.broadcasted_iota(jnp.int32, (16, DIM), 1)
    mine16, mine32 = rows(c * 16, 16), rows(c * 32, 32)
    both = jnp.where(lane < ROPE, small[1, even, :], small[1, odd, :])
    qa_all[mine32, :] = jnp.concatenate([small[0, even, :], both], axis=0).astype(BF16)
    qb_all[mine16, :] = small[0, odd, :].astype(BF16)
    counts[c] = jnp.zeros((1, DIM), F32) + count.astype(F32)

    pl.semaphore_wait(barrier, (NZ - 1) + (NX - 1) + (NHG - 1))

    q_parts = ((qa_all, 32), (qb_all, 16))

    def to_x(block, send_sem, x_sem):
        for j in (2, 1, 3):
            send(block, block, send_sem, x_sem, x_peer(j), g)

    for i, (ref, size) in enumerate(q_parts):
        block = ref.at[rows(c * size, size)]
        for k in FAR_FIRST:
            send(block, block, q_send.at[i], qz_recv.at[i, k], z_peer(k), g)
        send(block, block, q_send.at[i], q2_recv.at[i], x_peer(2), g)
        for j in (1, 3):
            send(block, block, q_send.at[i], qx_recv.at[i], x_peer(j), g)
        if i == 0:
            for k in FAR_FIRST:
                send(counts.at[c], counts.at[c], n_send, nz_recv, z_peer(k), g)

    loads[4].wait()
    wide[...] = upk_v[...].astype(F32).reshape(LAT * HD, DIM)
    for h in range(HD):
        wk[:, h * DIM : (h + 1) * DIM] = wide[pl.ds(h, LAT, stride=HD), :].astype(BF16)
    loads[5].wait()
    for h in range(0, HD, 2):
        two = jnp.dot(
            lat_v[...], wk[:, h * DIM : (h + 2) * DIM], preferred_element_type=F32
        ).astype(BF16)
        keys[h] = two[:, 0:DIM]
        keys[h + 1] = two[:, DIM:]

    loads[6].wait()
    wide[...] = upv_v[...].astype(F32).reshape(LAT * HD, DIM)
    for h in range(HD):
        wvt[h * DIM : (h + 1) * DIM, :] = wide[pl.ds(h, LAT, stride=HD), :].T.astype(BF16)
    for n in range(0, SLOTS, 256):
        values_t[:, n : n + 256] = lax.dot_general(
            wvt[...], lat_v[n : n + 256, :], (((1,), (1,)), ((), ())),
            preferred_element_type=F32,
        ).astype(BF16)
    loads[7].wait()
    rope = rope_v[...].astype(F32)
    blank = jnp.zeros((DIM - ROPE, SLOTS), F32)
    kr[0] = jnp.concatenate([rope, blank], axis=0).T.astype(BF16)
    kr[1] = jnp.concatenate([blank, rope], axis=0).T.astype(BF16)

    for i, (ref, size) in enumerate(q_parts):
        for k in NEAR_FIRST:
            block = ref.at[rows(z_peer(k) * size, size)]
            drain(block, qz_recv.at[i, NZ - k])
            for j in (1, 3) if NZ - k in VIA_X else (2, 1, 3):
                send(block, block, q_send.at[i], qx_recv.at[i], x_peer(j), g)
            if k == 6:
                across = ref.at[rows(x_peer(2) * size, size)]
                drain(across, q2_recv.at[i])
                for near in VIA_X:
                    send(across, across, q_send.at[i], qx_recv.at[i], z_peer(near), g)
        if i == 0:
            drain(counts.at[pl.ds(0, NZ - 1)], nz_recv)
            to_x(counts.at[rows(column, NZ)], n_send, nx_recv)

    drain(counts.at[pl.ds(0, 24)], nx_recv)
    shard = lax.broadcasted_iota(jnp.int32, (NCTX, DIM), 0)
    before = jnp.where(shard < c, counts[:, 0, :], 0.0)
    offset = jnp.sum(before, axis=0, keepdims=True).astype(jnp.int32)
    token = lax.broadcasted_iota(jnp.int32, (1, TOK), 1)
    limit = jnp.minimum(token + (span[0] + 1) - offset, count)
    slot = lax.broadcasted_iota(jnp.int32, (SLOTS, TOK), 0)

    def scores_of(i, t):
        p = lax.rem(x + 1 + t, NX)
        mine = pl.ds(p, TOK, stride=PAIRS)
        q = jnp.concatenate([q_wide[mine, :].astype(BF16), r_wide[mine, :].astype(BF16)], axis=1)
        k_cat = jnp.concatenate([keys[2 * p + i], kr[i]], axis=1)
        return lax.dot_general(k_cat, q, (((1,), (1,)), ((), ())), preferred_element_type=F32)

    def weights_of(i, t, scores):
        scores = jnp.where(slot < limit, scores, NEG)
        top = jnp.max(scores, axis=0, keepdims=True)
        weights = jnp.exp2((scores - top) * FACTOR2)
        total = jnp.sum(weights, axis=0, keepdims=True)
        lse_mine[i, lax.rem(x + 1 + t, NX)] = top * FACTOR2 + jnp.log(total) * LOG2E
        return weights.astype(BF16), 1.0 / total

    def values_of(i, t, weights, scale):
        p = lax.rem(x + 1 + t, NX)
        summed = jnp.dot(
            values_t[rows((2 * p + i) * DIM, DIM), :], weights, preferred_element_type=F32
        )
        o_mine[i, rows(p * DIM, DIM), :] = (summed * scale).astype(BF16)

    def give_out(i, t):
        p = lax.rem(x + 1 + t, NX)
        for zz in OWNER_ORDER[i]:
            dst = p * NZ + zz
            place = lax.rem(c - dst + NCTX, NCTX)
            mine = rows((p * 4 + zz // 2) * 32, 32)

            def go():
                send(lse_mine.at[i, p], lse_all.at[place], lse_send, lse_recv, dst, g)
                send(
                    o_mine.at[i, mine], o_all.at[rows(place * 32, 32)], o_send, o_recv, dst, g
                )

            if t < PAIRS - 1:
                go()
            else:
                pl.when(zz != z)(go)

    for i, (ref, size) in enumerate(q_parts):
        drain(ref.at[pl.ds(0, 23 * size)], qx_recv.at[i])
        got = ref[...].astype(F32).reshape(NCTX, size, DIM)
        q_wide[...] = got[:, 0:16].reshape(NCTX * 16, DIM)
        if i == 0:
            r_wide[...] = got[:, 16:32].reshape(NCTX * 16, DIM)
        coming = scores_of(i, 0)
        for t in range(PAIRS):
            scores = coming
            if t < PAIRS - 1:
                coming = scores_of(i, t + 1)
            values_of(i, t, *weights_of(i, t, scores))
            give_out(i, t)

    group, place = lax.rem(z, 2), x * 4 + lax.div(z, 2)
    own = rows(place * 32, 32)
    o_all[0:32, :] = o_mine[group, own, :]
    lse_all[0] = lse_mine[group, x]
    drain(lse_all.at[pl.ds(1, NCTX - 1)], lse_recv)
    lse = lse_all[:, 0, :]
    share = jnp.exp2(lse - jnp.max(lse, axis=0, keepdims=True))
    share = share / jnp.sum(share, axis=0, keepdims=True)
    drain(o_all.at[pl.ds(32, (NCTX - 1) * 32)], o_recv)
    joined = jnp.zeros((32, TOK), F32)
    for s in range(NCTX):
        joined = joined + o_all[s * 32 : (s + 1) * 32, :].astype(F32) * share[s : s + 1, :]
    a_all[group, own, :] = joined.astype(BF16)
    block = a_all.at[group, own]
    for zz in range(HOT):
        @pl.when(z != zz)
        def _():
            send(block, block, a_send, az_recv.at[z], column + zz, g)

        for j in (2, 1, 3):
            dst = lax.rem(column + NZ * j, NCTX) + zz
            send(block, block, a_send, ax_recv.at[group], dst, g)
    for k in FAR_FIRST:
        @pl.when(lax.rem(z + k, NZ) >= HOT)
        def _():
            send(block, block, a_send, az_recv.at[z], z_peer(k), g)

    @pl.when(z >= HOT)
    def _():
        to_x(block, a_send, ax_recv.at[group])

    def pass_on(k):
        zz = lax.rem(z + k, NZ)
        group = lax.rem(zz, 2)
        block = a_all.at[group, rows((x * 4 + lax.div(zz, 2)) * 32, 32)]
        drain(block, az_recv.at[zz])

        @pl.when(z >= HOT)
        def _():
            to_x(block, a_send, ax_recv.at[group])

    loads[8].wait()
    w = [jnp.concatenate([wt_v[2 * p + i] for p in range(PAIRS)], axis=1) for i in range(2)]
    for k in PASS_ORDER:
        pass_on(k)
    drain(a_all.at[0, pl.ds(0, 12 * 32)], ax_recv.at[0])
    mixed_t = jnp.dot(w[0], a_all[0], preferred_element_type=F32)
    drain(a_all.at[1, pl.ds(0, 12 * 32)], ax_recv.at[1])
    mixed_t = mixed_t + jnp.dot(w[1], a_all[1], preferred_element_type=F32)
    mixed_t = jnp.concatenate([mixed_t, jnp.zeros((256 - COLS, TOK), F32)], axis=0)
    left = mixed_t[0:128].T.reshape(NHG, 8, 128)
    right = mixed_t[128:].T.reshape(NHG, 8, 128)
    part[...] = jnp.concatenate([left, right], axis=1).astype(BF16).reshape(NHG * 16, 128)
    for dst in (0, 1, 8, 9, 6, 7, 10, 11, 4, 5, 12, 13, 2, 3, 14, 15):
        @pl.when(g != dst)
        def _():
            place = lax.rem(g - dst + NHG, NHG)
            send(
                part.at[dst * 16 : (dst + 1) * 16], part_all.at[rows(place * 16, 16)],
                p_send, p_recv, c, dst,
            )

    acc = part[rows(g * 16, 16), :].astype(F32)
    drain(part_all.at[pl.ds(16, (NHG - 1) * 16)], p_recv)
    for k in range(1, NHG):
        acc = acc + part_all[k * 16 : (k + 1) * 16, :].astype(F32)
    out[...] = jnp.concatenate([acc[0:8], acc[8:16, 0 : COLS - 128]], axis=1).astype(BF16)

    for i, (ref, size) in enumerate(q_parts):
        drain(ref.at[pl.ds(0, 31 * size)], q_send.at[i])
    drain(o_all.at[pl.ds(32, (NCTX - 1) * 32)], o_send)
    drain(lse_all.at[pl.ds(1, NCTX - 1)], lse_send)
    drain(o_all.at[pl.ds(0, (NZ - 1 + 3 * HOT) * 32)], a_send)

    @pl.when(z >= HOT)
    def _():
        drain(o_all.at[pl.ds(0, 24 * 32)], a_send)

    drain(counts.at[pl.ds(0, 31)], n_send)
    drain(part_all.at[pl.ds(16, (NHG - 1) * 16)], p_send)


def per_device(
    query_nope, query_rope, latent, key_rope, up_keys, up_values, out_weight, live_rows, span_start
):
    hbm = pl.BlockSpec(memory_space=pltpu.HBM)
    dma = pltpu.SemaphoreType.DMA
    call = pl.pallas_call(
        kernel,
        out_shape=jax.ShapeDtypeStruct((TOK // NHG, COLS), BF16),
        in_specs=[hbm] * 9,
        out_specs=pl.BlockSpec(memory_space=pltpu.VMEM),
        scratch_shapes=[
            pltpu.SMEM((1,), jnp.int32),
            pltpu.SMEM((1,), jnp.int32),
            pltpu.VMEM((4, HD, DIM), BF16),
            pltpu.VMEM((4, HD, ROPE), BF16),
            pltpu.VMEM((SLOTS, LAT), BF16),
            pltpu.VMEM((ROPE, SLOTS), BF16),
            pltpu.VMEM((LAT, HD, DIM), BF16),
            pltpu.VMEM((LAT, HD, DIM), BF16),
            pltpu.VMEM((HD, COLS, DIM), BF16),
            pltpu.VMEM((2, 4 * HD, DIM), F32),
            pltpu.VMEM((LAT * HD, DIM), F32),
            pltpu.VMEM((LAT, HD * DIM), BF16),
            pltpu.VMEM((HD * DIM, LAT), BF16),
            pltpu.VMEM((HD, SLOTS, DIM), BF16),
            pltpu.VMEM((HD * DIM, SLOTS), BF16),
            pltpu.VMEM((2, SLOTS, DIM), BF16),
            pltpu.VMEM((NCTX * 32, DIM), BF16),
            pltpu.VMEM((NCTX * 16, DIM), BF16),
            pltpu.VMEM((NCTX * 16, DIM), F32),
            pltpu.VMEM((NCTX * 16, DIM), F32),
            pltpu.VMEM((NCTX, 1, DIM), F32),
            pltpu.VMEM((2, PAIRS * DIM, TOK), BF16),
            pltpu.VMEM((2, PAIRS, 1, TOK), F32),
            pltpu.VMEM((NCTX * 32, TOK), BF16),
            pltpu.VMEM((NCTX, 1, TOK), F32),
            pltpu.VMEM((2, PAIRS * DIM, TOK), BF16),
            pltpu.VMEM((NHG * 16, 128), BF16),
            pltpu.VMEM((NHG * 16, 128), BF16),
            dma((9,)), dma((2,)), dma((2, NZ)), dma((2,)), dma((2,)), dma, dma, dma,
            dma, dma, dma, dma, dma, dma((NZ,)), dma((2,)), dma, dma,
        ],
        compiler_params=pltpu.CompilerParams(
            collective_id=0, has_side_effects=True, vmem_limit_bytes=48 * 1024 * 1024
        ),
    )
    large = (
        query_nope, query_rope, latent, key_rope.T, up_keys, up_values,
        jnp.transpose(out_weight, (0, 2, 1)),
    )
    return call(
        live_rows, span_start, *[pltpu.with_memory_space_constraint(a, pltpu.HBM) for a in large]
    )


def solution(mesh):
    placed = (
        P("ctx", "hg", None),
        P("ctx", "hg", None),
        P("ctx", None),
        P("ctx", None),
        P(None, "hg", None),
        P(None, "hg", None),
        P("hg", None, "ctx"),
        P("ctx"),
        P(),
    )
    return jax.shard_map(
        per_device, mesh=mesh, in_specs=placed, out_specs=P("hg", "ctx"), check_vma=False
    )
```

```python
import math

import jax
import jax.numpy as jnp
from jax import lax
from jax.experimental import pallas as pl
from jax.experimental.pallas import tpu as pltpu
from jax.sharding import PartitionSpec as P

NEG = -1e30
NCTX, NX, NZ, NHG = 32, 4, 8, 16
TOK, HD, DIM, ROPE, LAT, SLOTS, COLS = 128, 8, 128, 64, 512, 768, 224
PAIRS = HD // 2
LOG2E = math.log2(math.e)
FACTOR2 = LOG2E / math.sqrt(DIM + ROPE)
MESH = pl.DeviceIdType.MESH
F32, BF16 = jnp.float32, jnp.bfloat16
NEAR_FIRST = (1, 7, 2, 6, 3, 5, 4)
FAR_FIRST = (4, 3, 5, 2, 6, 1, 7)
HOT = 3
VIA_X = (1, 7, 2, 6)
OWNER_ORDER = ((4, 2, 6, 0), (3, 5, 1, 7))
PASS_ORDER = (1, 7, 2, 6, 3, 5, 4)


def rows(start, size):
    return pl.ds(pl.multiple_of(start, size), size)


def kernel(
    live_h, span_h, qn_h, qr_h, latent, rope_t, up_k, up_v, weight_t, out,
    live, span, qn, qr, lat_v, rope_v, upk_v, upv_v, wt_v, small, wide, wk, wvt,
    keys, values_t, kr, qa_all, qb_all, q_wide, r_wide, counts,
    o_mine, lse_mine, o_all, lse_all, a_all, part, part_all,
    load_sem, q_send, qz_recv, qx_recv, q2_recv, n_send, nz_recv, nx_recv,
    o_send, o_recv, lse_send, lse_recv, a_send, az_recv, ax_recv, p_send, p_recv,
):
    c, g = lax.axis_index("ctx"), lax.axis_index("hg")
    z, x = lax.rem(c, NZ), lax.div(c, NZ)
    column = x * NZ

    def z_peer(k):
        return column + lax.rem(z + k, NZ)

    def x_peer(k):
        return lax.rem(c + NZ * k, NCTX)

    def zx_peer(k, j):
        return lax.rem(z_peer(k) + NZ * j, NCTX)

    def h_peer(k):
        return lax.rem(g + k, NHG)

    def send(src, dst, send_sem, recv_sem, ctx, hg):
        pltpu.make_async_remote_copy(
            src_ref=src, dst_ref=dst, send_sem=send_sem, recv_sem=recv_sem,
            device_id=(ctx, hg), device_id_type=MESH,
        ).start()

    def drain(ref, sem):
        pltpu.make_async_copy(ref, ref, sem).wait()

    barrier = pltpu.get_barrier_semaphore()
    for k in FAR_FIRST:
        pl.semaphore_signal(barrier, inc=1, device_id=(z_peer(k), g), device_id_type=MESH)
    for k in range(1, NX):
        pl.semaphore_signal(barrier, inc=1, device_id=(x_peer(k), g), device_id_type=MESH)
    for k in range(1, NHG):
        pl.semaphore_signal(barrier, inc=1, device_id=(c, h_peer(k)), device_id_type=MESH)

    loads = [
        pltpu.make_async_copy(src, dst, load_sem.at[i])
        for i, (src, dst) in enumerate(
            (
                (live_h, live), (span_h, span), (qn_h, qn), (qr_h, qr),
                (up_k, upk_v), (latent, lat_v), (up_v, upv_v), (rope_t, rope_v), (weight_t, wt_v),
            )
        )
    ]
    for load in loads:
        load.start()
    for load in loads[:4]:
        load.wait()

    count = live[0]
    small[0] = qn[...].astype(F32).reshape(4 * HD, DIM)
    rope = qr[...].astype(F32).reshape(4 * HD, ROPE)
    small[1] = jnp.concatenate([rope, rope], axis=1)
    even, odd = pl.ds(0, 16, stride=2), pl.ds(1, 16, stride=2)
    lane = lax.broadcasted_iota(jnp.int32, (16, DIM), 1)
    mine16, mine32 = rows(c * 16, 16), rows(c * 32, 32)
    both = jnp.where(lane < ROPE, small[1, even, :], small[1, odd, :])
    qa_all[mine32, :] = jnp.concatenate([small[0, even, :], both], axis=0).astype(BF16)
    qb_all[mine16, :] = small[0, odd, :].astype(BF16)
    counts[c] = jnp.zeros((1, DIM), F32) + count.astype(F32)

    pl.semaphore_wait(barrier, (NZ - 1) + (NX - 1) + (NHG - 1))

    q_parts = ((qa_all, 32), (qb_all, 16))

    def to_x(block, send_sem, x_sem):
        for j in (2, 1, 3):
            send(block, block, send_sem, x_sem, x_peer(j), g)

    for i, (ref, size) in enumerate(q_parts):
        block = ref.at[rows(c * size, size)]
        for k in FAR_FIRST:
            send(block, block, q_send.at[i], qz_recv.at[i, k], z_peer(k), g)
        send(block, block, q_send.at[i], q2_recv.at[i], x_peer(2), g)
        for j in (1, 3):
            send(block, block, q_send.at[i], qx_recv.at[i], x_peer(j), g)
        if i == 0:
            for k in FAR_FIRST:
                send(counts.at[c], counts.at[c], n_send, nz_recv, z_peer(k), g)

    loads[4].wait()
    wide[...] = upk_v[...].astype(F32).reshape(LAT * HD, DIM)
    for h in range(HD):
        wk[:, h * DIM : (h + 1) * DIM] = wide[pl.ds(h, LAT, stride=HD), :].astype(BF16)
    loads[5].wait()
    for h in range(0, HD, 2):
        two = jnp.dot(
            lat_v[...], wk[:, h * DIM : (h + 2) * DIM], preferred_element_type=F32
        ).astype(BF16)
        keys[h] = two[:, 0:DIM]
        keys[h + 1] = two[:, DIM:]

    loads[6].wait()
    wide[...] = upv_v[...].astype(F32).reshape(LAT * HD, DIM)
    for h in range(HD):
        wvt[h * DIM : (h + 1) * DIM, :] = wide[pl.ds(h, LAT, stride=HD), :].T.astype(BF16)
    for n in range(0, SLOTS, 256):
        values_t[:, n : n + 256] = lax.dot_general(
            wvt[...], lat_v[n : n + 256, :], (((1,), (1,)), ((), ())),
            preferred_element_type=F32,
        ).astype(BF16)
    loads[7].wait()
    rope = rope_v[...].astype(F32)
    blank = jnp.zeros((DIM - ROPE, SLOTS), F32)
    kr[0] = jnp.concatenate([rope, blank], axis=0).T.astype(BF16)
    kr[1] = jnp.concatenate([blank, rope], axis=0).T.astype(BF16)

    for i, (ref, size) in enumerate(q_parts):
        for k in NEAR_FIRST:
            block = ref.at[rows(z_peer(k) * size, size)]
            drain(block, qz_recv.at[i, NZ - k])
            for j in (1, 3) if NZ - k in VIA_X else (2, 1, 3):
                send(block, block, q_send.at[i], qx_recv.at[i], x_peer(j), g)
            if k == 6:
                across = ref.at[rows(x_peer(2) * size, size)]
                drain(across, q2_recv.at[i])
                for near in VIA_X:
                    send(across, across, q_send.at[i], qx_recv.at[i], z_peer(near), g)
        if i == 0:
            drain(counts.at[pl.ds(0, NZ - 1)], nz_recv)
            to_x(counts.at[rows(column, NZ)], n_send, nx_recv)

    drain(counts.at[pl.ds(0, 24)], nx_recv)
    shard = lax.broadcasted_iota(jnp.int32, (NCTX, DIM), 0)
    before = jnp.where(shard < c, counts[:, 0, :], 0.0)
    offset = jnp.sum(before, axis=0, keepdims=True).astype(jnp.int32)
    token = lax.broadcasted_iota(jnp.int32, (1, TOK), 1)
    limit = jnp.minimum(token + (span[0] + 1) - offset, count)
    slot = lax.broadcasted_iota(jnp.int32, (SLOTS, TOK), 0)

    def scores_of(i, t):
        p = lax.rem(x + 1 + t, NX)
        mine = pl.ds(p, TOK, stride=PAIRS)
        q = jnp.concatenate([q_wide[mine, :].astype(BF16), r_wide[mine, :].astype(BF16)], axis=1)
        k_cat = jnp.concatenate([keys[2 * p + i], kr[i]], axis=1)
        return lax.dot_general(k_cat, q, (((1,), (1,)), ((), ())), preferred_element_type=F32)

    def weights_of(i, t, scores):
        scores = jnp.where(slot < limit, scores, NEG)
        top = jnp.max(scores, axis=0, keepdims=True)
        weights = jnp.exp2((scores - top) * FACTOR2)
        total = jnp.sum(weights, axis=0, keepdims=True)
        lse_mine[i, lax.rem(x + 1 + t, NX)] = top * FACTOR2 + jnp.log(total) * LOG2E
        return weights.astype(BF16), 1.0 / total

    def values_of(i, t, weights, scale):
        p = lax.rem(x + 1 + t, NX)
        summed = jnp.dot(
            values_t[rows((2 * p + i) * DIM, DIM), :], weights, preferred_element_type=F32
        )
        o_mine[i, rows(p * DIM, DIM), :] = (summed * scale).astype(BF16)

    def give_out(i, t):
        p = lax.rem(x + 1 + t, NX)
        for zz in OWNER_ORDER[i]:
            dst = p * NZ + zz
            place = lax.rem(c - dst + NCTX, NCTX)
            mine = rows((p * 4 + zz // 2) * 32, 32)

            def go():
                send(lse_mine.at[i, p], lse_all.at[place], lse_send, lse_recv, dst, g)
                send(
                    o_mine.at[i, mine], o_all.at[rows(place * 32, 32)], o_send, o_recv, dst, g
                )

            if t < PAIRS - 1:
                go()
            else:
                pl.when(zz != z)(go)

    for i, (ref, size) in enumerate(q_parts):
        drain(ref.at[pl.ds(0, 23 * size)], qx_recv.at[i])
        got = ref[...].astype(F32).reshape(NCTX, size, DIM)
        q_wide[...] = got[:, 0:16].reshape(NCTX * 16, DIM)
        if i == 0:
            r_wide[...] = got[:, 16:32].reshape(NCTX * 16, DIM)
        coming = scores_of(i, 0)
        for t in range(PAIRS):
            scores = coming
            if t < PAIRS - 1:
                coming = scores_of(i, t + 1)
            values_of(i, t, *weights_of(i, t, scores))
            give_out(i, t)

    group, place = lax.rem(z, 2), x * 4 + lax.div(z, 2)
    own = rows(place * 32, 32)
    o_all[0:32, :] = o_mine[group, own, :]
    lse_all[0] = lse_mine[group, x]
    drain(lse_all.at[pl.ds(1, NCTX - 1)], lse_recv)
    lse = lse_all[:, 0, :]
    share = jnp.exp2(lse - jnp.max(lse, axis=0, keepdims=True))
    share = share / jnp.sum(share, axis=0, keepdims=True)
    drain(o_all.at[pl.ds(32, (NCTX - 1) * 32)], o_recv)
    joined = jnp.zeros((32, TOK), F32)
    for s in range(NCTX):
        joined = joined + o_all[s * 32 : (s + 1) * 32, :].astype(F32) * share[s : s + 1, :]
    a_all[group, own, :] = joined.astype(BF16)
    block = a_all.at[group, own]
    for zz in range(HOT):
        @pl.when(z != zz)
        def _():
            send(block, block, a_send, az_recv.at[z], column + zz, g)

        for j in (2, 1, 3):
            dst = lax.rem(column + NZ * j, NCTX) + zz
            send(block, block, a_send, ax_recv.at[group], dst, g)
    for k in FAR_FIRST:
        @pl.when(lax.rem(z + k, NZ) >= HOT)
        def _():
            send(block, block, a_send, az_recv.at[z], z_peer(k), g)

    @pl.when(z >= HOT)
    def _():
        to_x(block, a_send, ax_recv.at[group])

    def pass_on(k):
        zz = lax.rem(z + k, NZ)
        group = lax.rem(zz, 2)
        block = a_all.at[group, rows((x * 4 + lax.div(zz, 2)) * 32, 32)]
        drain(block, az_recv.at[zz])

        @pl.when(z >= HOT)
        def _():
            to_x(block, a_send, ax_recv.at[group])

    loads[8].wait()
    w = [jnp.concatenate([wt_v[2 * p + i] for p in range(PAIRS)], axis=1) for i in range(2)]
    for k in PASS_ORDER:
        pass_on(k)
    drain(a_all.at[0, pl.ds(0, 12 * 32)], ax_recv.at[0])
    mixed_t = jnp.dot(w[0], a_all[0], preferred_element_type=F32)
    drain(a_all.at[1, pl.ds(0, 12 * 32)], ax_recv.at[1])
    mixed_t = mixed_t + jnp.dot(w[1], a_all[1], preferred_element_type=F32)
    mixed_t = jnp.concatenate([mixed_t, jnp.zeros((256 - COLS, TOK), F32)], axis=0)
    left = mixed_t[0:128].T.reshape(NHG, 8, 128)
    right = mixed_t[128:].T.reshape(NHG, 8, 128)
    part[...] = jnp.concatenate([left, right], axis=1).astype(BF16).reshape(NHG * 16, 128)
    for dst in (0, 1, 8, 9, 6, 7, 10, 11, 4, 5, 12, 13, 2, 3, 14, 15):
        @pl.when(g != dst)
        def _():
            place = lax.rem(g - dst + NHG, NHG)
            send(
                part.at[dst * 16 : (dst + 1) * 16], part_all.at[rows(place * 16, 16)],
                p_send, p_recv, c, dst,
            )

    acc = part[rows(g * 16, 16), :].astype(F32)
    drain(part_all.at[pl.ds(16, (NHG - 1) * 16)], p_recv)
    for k in range(1, NHG):
        acc = acc + part_all[k * 16 : (k + 1) * 16, :].astype(F32)
    out[...] = jnp.concatenate([acc[0:8], acc[8:16, 0 : COLS - 128]], axis=1).astype(BF16)

    for i, (ref, size) in enumerate(q_parts):
        drain(ref.at[pl.ds(0, 31 * size)], q_send.at[i])
    drain(o_all.at[pl.ds(32, (NCTX - 1) * 32)], o_send)
    drain(lse_all.at[pl.ds(1, NCTX - 1)], lse_send)
    drain(o_all.at[pl.ds(0, (NZ - 1 + 3 * HOT) * 32)], a_send)

    @pl.when(z >= HOT)
    def _():
        drain(o_all.at[pl.ds(0, 24 * 32)], a_send)

    drain(counts.at[pl.ds(0, 31)], n_send)
    drain(part_all.at[pl.ds(16, (NHG - 1) * 16)], p_send)


def per_device(
    query_nope, query_rope, latent, key_rope, up_keys, up_values, out_weight, live_rows, span_start
):
    hbm = pl.BlockSpec(memory_space=pltpu.HBM)
    dma = pltpu.SemaphoreType.DMA
    call = pl.pallas_call(
        kernel,
        out_shape=jax.ShapeDtypeStruct((TOK // NHG, COLS), BF16),
        in_specs=[hbm] * 9,
        out_specs=pl.BlockSpec(memory_space=pltpu.VMEM),
        scratch_shapes=[
            pltpu.SMEM((1,), jnp.int32),
            pltpu.SMEM((1,), jnp.int32),
            pltpu.VMEM((4, HD, DIM), BF16),
            pltpu.VMEM((4, HD, ROPE), BF16),
            pltpu.VMEM((SLOTS, LAT), BF16),
            pltpu.VMEM((ROPE, SLOTS), BF16),
            pltpu.VMEM((LAT, HD, DIM), BF16),
            pltpu.VMEM((LAT, HD, DIM), BF16),
            pltpu.VMEM((HD, COLS, DIM), BF16),
            pltpu.VMEM((2, 4 * HD, DIM), F32),
            pltpu.VMEM((LAT * HD, DIM), F32),
            pltpu.VMEM((LAT, HD * DIM), BF16),
            pltpu.VMEM((HD * DIM, LAT), BF16),
            pltpu.VMEM((HD, SLOTS, DIM), BF16),
            pltpu.VMEM((HD * DIM, SLOTS), BF16),
            pltpu.VMEM((2, SLOTS, DIM), BF16),
            pltpu.VMEM((NCTX * 32, DIM), BF16),
            pltpu.VMEM((NCTX * 16, DIM), BF16),
            pltpu.VMEM((NCTX * 16, DIM), F32),
            pltpu.VMEM((NCTX * 16, DIM), F32),
            pltpu.VMEM((NCTX, 1, DIM), F32),
            pltpu.VMEM((2, PAIRS * DIM, TOK), BF16),
            pltpu.VMEM((2, PAIRS, 1, TOK), F32),
            pltpu.VMEM((NCTX * 32, TOK), BF16),
            pltpu.VMEM((NCTX, 1, TOK), F32),
            pltpu.VMEM((2, PAIRS * DIM, TOK), BF16),
            pltpu.VMEM((NHG * 16, 128), BF16),
            pltpu.VMEM((NHG * 16, 128), BF16),
            dma((9,)), dma((2,)), dma((2, NZ)), dma((2,)), dma((2,)), dma, dma, dma,
            dma, dma, dma, dma, dma, dma((NZ,)), dma((2,)), dma, dma,
        ],
        compiler_params=pltpu.CompilerParams(
            collective_id=0, has_side_effects=True, vmem_limit_bytes=48 * 1024 * 1024
        ),
    )
    large = (
        query_nope, query_rope, latent, key_rope.T, up_keys, up_values,
        jnp.transpose(out_weight, (0, 2, 1)),
    )
    return call(
        live_rows, span_start, *[pltpu.with_memory_space_constraint(a, pltpu.HBM) for a in large]
    )


def solution(mesh):
    placed = (
        P("ctx", "hg", None),
        P("ctx", "hg", None),
        P("ctx", None),
        P("ctx", None),
        P(None, "hg", None),
        P(None, "hg", None),
        P("hg", None, "ctx"),
        P("ctx"),
        P(),
    )
    return jax.shard_map(
        per_device, mesh=mesh, in_specs=placed, out_specs=P("hg", "ctx"), check_vma=False
    )
```
